32 devices in a mesh: dp: 8 (over y, x, core), tensor: 4 (over z).
Axes of the slice: x: 2, y: 2, z: 4, core: 2. Of those that a mesh axis runs over, the one named last changes fastest.
Arguments:
- tokens: bfloat16 [8192, 1536], P(('dp', 'tensor')), may hold values from -6 to 6
- clip_ids: int32 [8192], P('dp'), may hold values from 0 to 2, as said below
- positions: int32 [8192], P('dp'), may hold values from 0 to 2047, as said below
- timesteps: int32 [24], P('dp'), may hold values from 0 to 999
- text_states: bfloat16 [24, 128, 4096], P('dp'), may hold values from -6 to 6
- text_lengths: int32 [24], P('dp'), may hold values from 1 to 128
- out_grad: bfloat16 [8192, 1536], P(('dp', 'tensor')), may hold values from -6 to 6
- attn_gain: float32 [1536], replicated, may hold values from 0.5 to 1.5
- ffn_gain: float32 [1536], replicated, may hold values from 0.5 to 1.5
- query_gain: float32 [64], replicated, may hold values from 0.5 to 1.5
- key_gain: float32 [64], replicated, may hold values from 0.5 to 1.5
- cross_gate: float32 [24], replicated, may hold values from 0.3 to 1.5
- w_query: bfloat16 [1536, 1536], P(None, 'tensor'), may hold values from -0.15625 to 0.15625
- w_key: bfloat16 [1536, 1536], P(None, 'tensor'), may hold values from -0.15625 to 0.15625
- w_value: bfloat16 [1536, 1536], P(None, 'tensor'), may hold values from -0.15625 to 0.15625
- w_out: bfloat16 [1536, 1536], P('tensor'), may hold values from -1.25 to 1.25
- w_text_key: bfloat16 [4096, 1536], P(None, 'tensor'), may hold values from -0.09375 to 0.09375
- w_text_value: bfloat16 [4096, 1536], P(None, 'tensor'), may hold values from -0.09375 to 0.09375
- w_ada: bfloat16 [1024, 6144], P(None, 'tensor'), may hold values from -0.1875 to 0.1875
- w_gate: bfloat16 [1536, 4096], P(None, 'tensor'), may hold values from -0.15625 to 0.15625
- w_up: bfloat16 [1536, 4096], P(None, 'tensor'), may hold values from -0.15625 to 0.15625
- w_down: bfloat16 [4096, 1536], P('tensor'), may hold values from -0.09375 to 0.09375
Outputs:
- block_out: bfloat16 [8192, 1536], P(('dp', 'tensor'))
- input_grad: float32 [8192, 1536], P(('dp', 'tensor'))
- attn_gain_grad: float32 [1536], replicated
- ffn_gain_grad: float32 [1536], replicated
- query_gain_grad: float32 [64], replicated
- key_gain_grad: float32 [64], replicated
- cross_gate_grad: float32 [24], replicated
- w_query_grad: float32 [1536, 1536], P('dp', 'tensor')
- w_key_grad: float32 [1536, 1536], P('dp', 'tensor')
- w_value_grad: float32 [1536, 1536], P('dp', 'tensor')
- w_out_grad: float32 [1536, 1536], P('tensor', 'dp')
- w_text_key_grad: float32 [4096, 1536], P('dp', 'tensor')
- w_text_value_grad: float32 [4096, 1536], P('dp', 'tensor')
- w_ada_grad: float32 [1024, 6144], P('dp', 'tensor')
- w_gate_grad: float32 [1536, 4096], P('dp', 'tensor')
- w_up_grad: float32 [1536, 4096], P('dp', 'tensor')
- w_down_grad: float32 [4096, 1536], P('tensor', 'dp')
The draws below stay inside these ranges and needn't reach their ends.
Inputs may be any that keep to these rules, and one draw needn't show every extreme that they name: `clip_ids`: in each aligned block of 1024 tokens the clip numbers never fall, and 0, 1 and 2 each occur; clips 0 and 2 each hold fewer than 256 tokens. Within a clip the positions rise by one from token to token.
All inputs are finite; a program needn't handle non-finite values.
Results may differ from the reference program's by a relative error of at most 0.015.
Values may be sent and summed in bfloat16 or wider, within the bound.
No kernel may reach another device: no remote copies, remote signals or barrier semaphores. Data moves between devices by JAX's collectives and lax.ppermute only.
A program may use at most 256 MiB of HBM per device.

```python
import math
from functools import partial
import jax
import jax.numpy as jnp
from jax import lax

D = 1536
HEADS = 24
HEAD_DIM = 64
FF = 4096
TEXT_DIM = 4096
COND = 1024
TEXT_LEN = 128
CLIPS = 3
ROWS = 256
GROUP = 1024
TOKENS = 8192
CLIPS_ALL = 24


def clip_bounds(key):
    group_count = TOKENS // GROUP
    front_key, tail_key = jax.random.split(key)
    front_len = jax.random.randint(front_key, (group_count,), 1, ROWS)
    tail_len = jax.random.randint(tail_key, (group_count,), 1, ROWS)
    places = jnp.arange(GROUP, dtype=jnp.int32)[None, :]
    second_start = GROUP - tail_len
    clip_rows = (places >= front_len[:, None]).astype(jnp.int32) + (places >= second_start[:, None]).astype(jnp.int32)
    return (front_len, second_start, clip_rows)


def draw_clip_ids(key, part):
    front_len, second_start, clip_rows = clip_bounds(key)
    return clip_rows.reshape(-1)


def draw_positions(key, part):
    front_len, second_start, clip_rows = clip_bounds(key)
    key = jax.random.fold_in(key, 12)
    group_count = TOKENS // GROUP
    last_start = jax.random.randint(key, (group_count,), 0, GROUP)
    middle_len = second_start - front_len
    middle_start = 2 * GROUP - middle_len
    starts = jnp.stack([jnp.zeros((group_count,), jnp.int32), middle_start.astype(jnp.int32), last_start.astype(jnp.int32)], axis=1)
    places = jnp.arange(GROUP, dtype=jnp.int32)[None, :]
    begins = jnp.where(clip_rows == 0, 0, jnp.where(clip_rows == 1, front_len[:, None], second_start[:, None]))
    offsets = jnp.take_along_axis(starts, clip_rows, axis=1)
    return (offsets + places - begins).astype(jnp.int32).reshape(-1)


def plant(drawn, stream_key, low, top_value):
    place = [jax.random.randint(jax.random.fold_in(stream_key, axis), (), 0, length) for axis, length in enumerate(drawn.shape)]
    main_axis = drawn.shape.index(max(drawn.shape))
    neighbour = place[:main_axis] + [(place[main_axis] + 1) % drawn.shape[main_axis]] + place[main_axis + 1:]
    return drawn.at[tuple(place)].set(low).at[tuple(neighbour)].set(top_value)


def shard_levels(stream_key, shape, cuts, smallest, high):
    loudness = 1.0
    for axis_at, blocks in cuts:
        heights = jax.random.uniform(jax.random.fold_in(jax.random.fold_in(stream_key, 6), axis_at), (blocks,), jnp.float32, smallest / len(cuts), high / len(cuts))
        loudness = loudness * jnp.repeat(jnp.exp(heights), shape[axis_at] // blocks).reshape((-1,) + (1,) * (len(shape) - 1 - axis_at))
    return loudness


def bell_draw(own_key, shape, width, limit, shards=(), kind=jnp.bfloat16):
    gain = shard_levels(own_key, shape, shards, -0.22, 0.18) if shards else 1.0
    drawn = jax.random.normal(own_key, shape, jnp.float32) * width * gain
    return jnp.minimum(jnp.maximum(drawn, -limit), limit).astype(kind)


def setup_inputs(seed: int = 0) -> dict:
    streams_of = jax.random.split(jax.random.key(seed), 23)
    return {
        "tokens": bell_draw(streams_of[0], (TOKENS, D), 1.0, 6.0, ((0, 32),)),
        "clip_ids": draw_clip_ids(jax.random.fold_in(streams_of[22], 71), 0),
        "positions": draw_positions(jax.random.fold_in(streams_of[22], 71), 0),
        "timesteps": plant(jax.random.randint(streams_of[3], (CLIPS_ALL,), 0, 1000), jax.random.fold_in(streams_of[3], 1), 0, 999).astype(jnp.int32),
        "text_states": bell_draw(streams_of[4], (CLIPS_ALL, TEXT_LEN, TEXT_DIM), 1.0, 6.0, ((0, 8),)),
        "text_lengths": plant(jax.random.randint(streams_of[5], (CLIPS_ALL,), 1, TEXT_LEN + 1), jax.random.fold_in(streams_of[5], 1), 1, TEXT_LEN).astype(jnp.int32),
        "out_grad": bell_draw(streams_of[6], (TOKENS, D), 1.0, 6.0, ((0, 32),)),
        "attn_gain": jnp.clip(1.0 + 0.1 * jax.random.normal(streams_of[7], (D,), jnp.float32), 0.5, 1.5),
        "ffn_gain": jnp.clip(1.0 + 0.1 * jax.random.normal(streams_of[8], (D,), jnp.float32), 0.5, 1.5),
        "query_gain": jnp.clip(1.0 + 0.1 * jax.random.normal(streams_of[9], (HEAD_DIM,), jnp.float32), 0.5, 1.5),
        "key_gain": jnp.clip(1.0 + 0.1 * jax.random.normal(streams_of[10], (HEAD_DIM,), jnp.float32), 0.5, 1.5),
        "cross_gate": jnp.clip(jax.random.uniform(streams_of[11], (HEADS,), jnp.float32, 0.3, 1.5), 0.3, 1.5),
        "w_query": bell_draw(streams_of[12], (D, D), D ** -0.5, 0.15625, ((1, 4),)),
        "w_key": bell_draw(streams_of[13], (D, D), D ** -0.5, 0.15625, ((1, 4),)),
        "w_value": bell_draw(streams_of[14], (D, D), D ** -0.5, 0.15625, ((1, 4),)),
        "w_out": bell_draw(streams_of[15], (D, D), (D // 64) ** -0.5, 1.25, ((0, 4),)),
        "w_text_key": bell_draw(streams_of[16], (TEXT_DIM, D), TEXT_DIM ** -0.5, 0.09375, ((1, 4),)),
        "w_text_value": bell_draw(streams_of[17], (TEXT_DIM, D), TEXT_DIM ** -0.5, 0.09375, ((1, 4),)),
        "w_ada": bell_draw(streams_of[18], (COND, 4 * D), COND ** -0.5, 0.1875, ((1, 4),)),
        "w_gate": bell_draw(streams_of[19], (D, FF), D ** -0.5, 0.15625, ((1, 4),)),
        "w_up": bell_draw(streams_of[20], (D, FF), D ** -0.5, 0.15625, ((1, 4),)),
        "w_down": bell_draw(streams_of[21], (FF, D), FF ** -0.5, 0.09375, ((0, 4),)),
    }


epsilon = 1e-06
masked_score = -1e+30

@jax.custom_vjp
def low(v):
    return lax.optimization_barrier(v.astype(jnp.bfloat16)).astype(jnp.float32)

@jax.custom_vjp
def low_back(v):
    return v

def low_keep(v):
    return (low(v), None)

def low_pass(kept, grad):
    return (grad,)

def back_keep(v):
    return (v, None)

def back_low(kept, grad):
    return (low(grad),)
low.defvjp(low_keep, low_pass)
low_back.defvjp(back_keep, back_low)

def matmul(left_side, right_side):
    return jnp.dot(left_side, right_side, precision=lax.Precision.HIGHEST)

def rms_scale(values):
    return lax.rsqrt(lax.optimization_barrier(jnp.mean(values * values, axis=-1, keepdims=True)) + epsilon)

def sigmoid_linear(values):
    return values * jax.nn.sigmoid(values)

def time_embed(time_steps, embed_width):
    half_width = embed_width // 2
    frequency = jnp.exp(-math.log(10000.0) * jnp.arange(half_width, dtype=jnp.float32) / half_width)
    angles = time_steps.astype(jnp.float32)[:, None] * frequency[None, :]
    return jnp.concatenate([jnp.cos(angles), jnp.sin(angles)], axis=-1)

def rotary(values, places, direction):
    head_width = values.shape[-1]
    half_width = head_width // 2
    frequency = jnp.exp(-math.log(10000.0) * jnp.arange(half_width, dtype=jnp.float32) * 2.0 / head_width)
    angles = places.astype(jnp.float32)[:, None] * frequency[None, :]
    cosine = jnp.cos(angles)[:, None, :]
    sine_part = direction * jnp.sin(angles)[:, None, :]
    lead_part = values[..., :half_width]
    tail_part = values[..., half_width:]
    return jnp.concatenate([lead_part * cosine - tail_part * sine_part, lead_part * sine_part + tail_part * cosine], axis=-1)

def clip_table(clip_rows, clip_count):
    return (clip_rows[:, None] == jnp.arange(clip_count, dtype=jnp.int32)[None, :]).astype(jnp.float32)

def softmax_rows(scores):
    shifted = scores - lax.optimization_barrier(jnp.max(scores, axis=-1, keepdims=True))
    exponent = jnp.exp(shifted)
    return exponent / lax.optimization_barrier(jnp.sum(exponent, axis=-1, keepdims=True))

def head_attend(clip_rows, text_owner, text_live, pieces):
    query_rows, key_rows, value_rows, text_keys, text_values, gate_value = pieces
    factor = 1.0 / math.sqrt(HEAD_DIM)
    same_clip = clip_rows[:, None] == clip_rows[None, :]
    self_scores = low_back(matmul(query_rows, key_rows.T) * factor)
    self_weights = softmax_rows(jnp.where(same_clip, self_scores, masked_score))
    self_out = low_back(matmul(low(self_weights), value_rows))
    allowed = (clip_rows[:, None] == text_owner[None, :]) & text_live[None, :]
    cross_scores = low_back(matmul(query_rows, text_keys.T) * factor)
    cross_weights = softmax_rows(jnp.where(allowed, cross_scores, masked_score))
    cross_out = low_back(matmul(low(cross_weights), text_values))
    return low(self_out + jnp.tanh(gate_value) * cross_out)

def group_forward(params, items):
    attn_gain, ffn_gain, query_gain, key_gain, cross_gate, w_query, w_key, w_value, w_out, w_text_key, w_text_value, w_ada, w_gate, w_up, w_down = params
    inputs, clip_rows, places, time_steps, text_block, text_lens = items
    condition = low(sigmoid_linear(time_embed(time_steps, COND)))
    modulation = low_back(matmul(condition, w_ada))
    per_token = matmul(clip_table(clip_rows, CLIPS), modulation)
    scale_attn = per_token[:, :D]
    gate_attn = jnp.tanh(per_token[:, D:2 * D])
    scale_ffn = per_token[:, 2 * D:3 * D]
    gate_ffn = jnp.tanh(per_token[:, 3 * D:])
    attn_rows = low(inputs * rms_scale(inputs) * attn_gain * (1.0 + scale_attn))
    head_shape = (GROUP, HEADS, HEAD_DIM)
    queries = low_back(matmul(attn_rows, w_query)).reshape(head_shape)
    key_raw = low_back(matmul(attn_rows, w_key)).reshape(head_shape)
    value_low = low(low_back(matmul(attn_rows, w_value))).reshape(head_shape)
    query_rot = low(rotary(queries * rms_scale(queries) * query_gain, places, 1.0))
    key_rot = low(rotary(key_raw * rms_scale(key_raw) * key_gain, places, 1.0))
    text_flat = text_block.reshape(CLIPS * TEXT_LEN, TEXT_DIM)
    text_shape = (CLIPS * TEXT_LEN, HEADS, HEAD_DIM)
    text_keys = low_back(matmul(text_flat, w_text_key)).reshape(text_shape)
    text_key_low = low(text_keys * rms_scale(text_keys) * key_gain)
    text_value_low = low(low_back(matmul(text_flat, w_text_value))).reshape(text_shape)
    text_owner = jnp.repeat(jnp.arange(CLIPS, dtype=jnp.int32), TEXT_LEN)
    text_live = jnp.tile(jnp.arange(TEXT_LEN, dtype=jnp.int32), CLIPS) < jnp.repeat(text_lens, TEXT_LEN)
    attend = jax.checkpoint(partial(head_attend, clip_rows, text_owner, text_live))
    mixed_heads = lax.map(attend, (jnp.swapaxes(query_rot, 0, 1), jnp.swapaxes(key_rot, 0, 1), jnp.swapaxes(value_low, 0, 1), jnp.swapaxes(text_key_low, 0, 1), jnp.swapaxes(text_value_low, 0, 1), cross_gate))
    mixed_heads = jnp.swapaxes(mixed_heads, 0, 1).reshape(GROUP, D)
    attn_out = low_back(matmul(mixed_heads, w_out))
    middle = inputs + gate_attn * attn_out
    ffn_rows = low(middle * rms_scale(middle) * ffn_gain * (1.0 + scale_ffn))
    gate_pre = low_back(matmul(ffn_rows, w_gate))
    up_pre = low_back(matmul(ffn_rows, w_up))
    hidden = low(sigmoid_linear(gate_pre) * up_pre)
    ffn_out = low_back(matmul(hidden, w_down))
    return middle + gate_ffn * ffn_out

def reference(tokens, clip_ids, positions, timesteps, text_states, text_lengths, out_grad, attn_gain, ffn_gain, query_gain, key_gain, cross_gate, w_query, w_key, w_value, w_out, w_text_key, w_text_value, w_ada, w_gate, w_up, w_down):
    group_count = TOKENS // GROUP
    params = tuple((element.astype(jnp.float32) for element in (attn_gain, ffn_gain, query_gain, key_gain, cross_gate, w_query, w_key, w_value, w_out, w_text_key, w_text_value, w_ada, w_gate, w_up, w_down)))
    fixed_items = (clip_ids.reshape(group_count, GROUP), positions.reshape(group_count, GROUP), timesteps.reshape(group_count, CLIPS), text_states.astype(jnp.float32).reshape(group_count, CLIPS, TEXT_LEN, TEXT_DIM), text_lengths.reshape(group_count, CLIPS))

    def forward(inputs, weights):

        def one_group(carried, items):
            return (carried, group_forward(weights, items))
        _, outputs = lax.scan(one_group, None, (inputs.reshape(group_count, GROUP, D),) + fixed_items)
        return outputs.reshape(TOKENS, D)
    outputs, pull = jax.vjp(forward, tokens.astype(jnp.float32), params)
    input_grad, grads = pull(out_grad.astype(jnp.float32))
    return (outputs.astype(jnp.bfloat16), input_grad, grads[0], grads[1], grads[2], grads[3], grads[4], grads[5], grads[6], grads[7], grads[8], grads[9], grads[10], grads[11], grads[12], grads[13], grads[14])
```

```python
import functools
import math

import jax
import jax.numpy as jnp
from jax import lax
from jax.experimental import pallas as pl
from jax.experimental.pallas import tpu as pltpu
from jax.sharding import PartitionSpec as P

epsilon = 1e-06
edge_rows = 256
apart = 2048.0


def rms_scale(values):
    return lax.rsqrt(jnp.mean(values * values, axis=-1, keepdims=True) + epsilon)


def rms_backward(grad_hat, normed, scaling):
    return scaling * (grad_hat - normed * jnp.mean(grad_hat * normed, axis=-1, keepdims=True))


def time_embed(time_steps, embed_width):
    half_width = embed_width // 2
    frequency = jnp.exp(-math.log(10000.0) * jnp.arange(half_width, dtype=jnp.float32) / half_width)
    angles = time_steps.astype(jnp.float32)[:, None] * frequency[None, :]
    return jnp.concatenate([jnp.cos(angles), jnp.sin(angles)], axis=-1)


def clip_table(clip_rows, clip_count):
    return (clip_rows[:, None] == jnp.arange(clip_count, dtype=jnp.int32)[None, :]).astype(
        jnp.float32
    )


def exchange(values, axis_name, distance):
    count = lax.axis_size(axis_name)
    return lax.ppermute(values, axis_name, [(i, i ^ distance) for i in range(count)])


def butterfly_sum(values):
    for axis_name in ("tensor", "dp"):
        count = lax.axis_size(axis_name)
        distance = 1
        while distance < count:
            values = values + exchange(values, axis_name, distance)
            distance *= 2
    return values


def halve(blocks, bit, axis_at):
    mine = (lax.axis_index("dp") >> bit) & 1
    given = lax.dynamic_index_in_dim(blocks, 1 - mine, axis_at, keepdims=False)
    kept = lax.dynamic_index_in_dim(blocks, mine, axis_at, keepdims=False)
    taken = exchange(given, "dp", 1 << bit)
    return kept.astype(jnp.float32) + taken.astype(jnp.float32)


def scatter_groups(partial_sum):
    count = lax.axis_size("dp")
    bits = count.bit_length() - 1
    rows, columns = partial_sum.shape
    blocks = partial_sum.reshape((2,) * bits + (rows // count, columns))
    blocks = halve(blocks, 0, bits - 1).astype(jnp.bfloat16)
    middle_col = columns // 2
    results = []
    for order, low_col in ((range(1, bits), 0), (range(bits - 1, 0, -1), middle_col)):
        part = blocks[..., low_col : low_col + middle_col]
        left = list(range(bits - 1, 0, -1))
        for step, bit in enumerate(order):
            part = halve(part, bit, left.index(bit))
            left.remove(bit)
            if step < bits - 2:
                part = part.astype(jnp.bfloat16)
        results.append(part)
    return jnp.concatenate(results, axis=-1)


def spread_groups(rows):
    count = lax.axis_size("dp")
    distance = 1
    rows = rows[None]
    while distance < count:
        other = exchange(rows, "dp", distance)
        mine = (lax.axis_index("dp") // distance) % 2
        first = jnp.where(mine == 0, rows, other)
        second = jnp.where(mine == 0, other, rows)
        rows = jnp.concatenate([first, second], axis=0)
        distance *= 2
    return rows


def scatter_rows(values):
    return lax.psum_scatter(
        values.astype(jnp.bfloat16), "tensor", scatter_dimension=0, tiled=True
    ).astype(jnp.float32)


def product(left, right, contract=((1,), (0,))):
    return lax.dot_general(left, right, (contract, ((), ())), preferred_element_type=jnp.float32)


def head_norm(raw):
    return lax.rsqrt(jnp.mean(raw * raw, axis=0, keepdims=True) + epsilon)


def turn(values, cosine, sine):
    half = values.shape[0] // 2
    lead, tail = values[:half], values[half:]
    return jnp.concatenate([lead * cosine - tail * sine, lead * sine + tail * cosine], axis=0)


def turn_back(values, cosine, sine):
    half = values.shape[0] // 2
    lead, tail = values[:half], values[half:]
    return jnp.concatenate([lead * cosine + tail * sine, tail * cosine - lead * sine], axis=0)


def widen(values, extra):
    rows = values.shape[0] + extra.shape[0]
    pad = jnp.zeros((128 - rows, values.shape[1]), values.dtype)
    return jnp.concatenate([values, extra.astype(values.dtype), pad], axis=0)


def text_range(block, blocks, clips, slots):
    first = 0 if block == 0 else slots
    last = (clips if block == blocks - 1 else clips - 1) * slots
    return first, last


def attend_forward(
    clips, slots, gates, query, key, value, text_key, text_value, table, text_table, cosine, sine,
    query_gain, key_gain, mixed, self_out, cross_out, self_inverse, cross_inverse,
):
    head_dim, rows = query.shape
    scale = math.log2(math.e) / math.sqrt(head_dim)
    gate = gates[pl.program_id(0)]
    raw = query[...]
    query_rot = turn(raw * head_norm(raw) * query_gain[...], cosine[...], sine[...])
    query_wide = widen(query_rot, table[0]).astype(jnp.bfloat16)
    raw = key[...]
    key_rot = turn(raw * head_norm(raw) * key_gain[...], cosine[...], sine[...])
    key_wide = widen(key_rot, table[1]).T.astype(jnp.bfloat16)
    raw = text_key[...]
    text_wide = widen(raw * head_norm(raw) * key_gain[...], text_table[...]).T.astype(jnp.bfloat16)
    ones_row = (lax.broadcasted_iota(jnp.int32, (16, rows), 0) == 0).astype(jnp.float32)
    value_wide = jnp.concatenate([value[...], ones_row], axis=0).astype(jnp.bfloat16)
    text_value_wide = jnp.concatenate(
        [text_value[...], ones_row[:, : text_value.shape[1]]], axis=0
    ).astype(jnp.bfloat16)
    blocks = rows // edge_rows
    for block in range(blocks):
        cols = slice(block * edge_rows, (block + 1) * edge_rows)
        query_blk = query_wide[:, cols]
        weights = jnp.exp2(product(key_wide, query_blk) * scale).astype(jnp.bfloat16)
        total = product(value_wide, weights)
        inverse = 1.0 / total[head_dim : head_dim + 1]
        own = total[:head_dim] * inverse
        first, last = text_range(block, blocks, clips, slots)
        weights = jnp.exp2(product(text_wide[first:last], query_blk) * scale).astype(jnp.bfloat16)
        total = product(text_value_wide[:, first:last], weights)
        text_inverse = 1.0 / total[head_dim : head_dim + 1]
        other = total[:head_dim] * text_inverse
        mixed[:, cols] = (own + gate * other).astype(jnp.bfloat16)
        self_out[:, cols] = own
        cross_out[:, cols] = other
        self_inverse[0, :, cols] = inverse
        cross_inverse[0, :, cols] = text_inverse


def attend_backward(
    clips, slots, gates, query, key, value, text_key, text_value, table, text_table, cosine, sine,
    query_gain, key_gain, grad, self_out, cross_out, self_inverse, cross_inverse,
    grad_qkv, grad_text, gain_sums, grad_key_sum, grad_value_sum, grad_query_all, text_key_sum, text_value_sum,
):
    head_dim, rows = query.shape
    scale = math.log2(math.e) / math.sqrt(head_dim)
    factor = 1.0 / math.sqrt(head_dim)
    gate = gates[pl.program_id(0)]
    raw = query[...]
    query_inv = head_norm(raw)
    query_rot = turn(raw * query_inv * query_gain[...], cosine[...], sine[...])
    query_wide = widen(query_rot, table[0]).astype(jnp.bfloat16)
    raw = key[...]
    key_inv = head_norm(raw)
    key_rot = turn(raw * key_inv * key_gain[...], cosine[...], sine[...])
    key_low = key_rot.astype(jnp.bfloat16)
    key_wide = widen(key_rot, table[1]).T.astype(jnp.bfloat16)
    raw = text_key[...]
    text_inv = head_norm(raw)
    text_norm = raw * text_inv * key_gain[...]
    text_low = text_norm.astype(jnp.bfloat16)
    text_wide = widen(text_norm, text_table[...]).T.astype(jnp.bfloat16)
    two_rows = (lax.broadcasted_iota(jnp.int32, (16, rows), 0) < 2).astype(jnp.float32)
    value_wide = widen(value[...], two_rows).T.astype(jnp.bfloat16)
    text_value_wide = widen(text_value[...], two_rows[:, : text_value.shape[1]]).T.astype(jnp.bfloat16)

    grads = grad[...].astype(jnp.float32)

    def with_dots(weighted, out):
        low = weighted.astype(jnp.bfloat16)
        dots = jnp.sum(low.astype(jnp.float32) * out, axis=0, keepdims=True)
        high = dots.astype(jnp.bfloat16).astype(jnp.float32)
        rows_at = lax.broadcasted_iota(jnp.int32, (16, rows), 0)
        extra = jnp.where(rows_at == 0, -high, jnp.where(rows_at == 1, high - dots, 0.0))
        return widen(low.astype(jnp.float32), extra).astype(jnp.bfloat16)

    self_wide = with_dots(grads * self_inverse[0], self_out[...])
    cross_wide = with_dots(grads * (gate * cross_inverse[0]), cross_out[...])
    blocks = rows // edge_rows
    text_key_sum[...] = jnp.zeros_like(text_key_sum)
    text_value_sum[...] = jnp.zeros_like(text_value_sum)
    for block in range(blocks):
        cols = slice(block * edge_rows, (block + 1) * edge_rows)
        query_blk = query_wide[:, cols]
        grad_blk = self_wide[:, cols]
        weights = jnp.exp2(product(key_wide, query_blk) * scale)
        slopes = (weights * product(value_wide, grad_blk)).astype(jnp.bfloat16)
        value_term = product(grad_blk[:head_dim], weights.astype(jnp.bfloat16), ((1,), (1,)))
        key_term = product(query_blk[:head_dim], slopes, ((1,), (1,)))
        if block == 0:
            grad_value_sum[...] = value_term
            grad_key_sum[...] = key_term
        else:
            grad_value_sum[...] += value_term
            grad_key_sum[...] += key_term
        query_term = product(key_low, slopes)
        first, last = text_range(block, blocks, clips, slots)
        grad_blk = cross_wide[:, cols]
        weights = jnp.exp2(product(text_wide[first:last], query_blk) * scale)
        slopes = (weights * product(text_value_wide[first:last], grad_blk)).astype(jnp.bfloat16)
        text_value_sum[:, first:last] += product(
            grad_blk[:head_dim], weights.astype(jnp.bfloat16), ((1,), (1,))
        )
        text_key_sum[:, first:last] += product(query_blk[:head_dim], slopes, ((1,), (1,)))
        grad_query_all[:, cols] = query_term + product(text_low[:, first:last], slopes)

    def through_norm(incoming, raw, inverse, gain):
        normed = raw * inverse
        scaled = incoming * gain
        mean = jnp.mean(scaled * normed, axis=0, keepdims=True)
        gain_part = jnp.sum(incoming * normed, axis=1, keepdims=True)
        return inverse * (scaled - normed * mean), gain_part

    incoming = turn_back(grad_query_all[...] * factor, cosine[...], sine[...])
    result, query_part = through_norm(incoming, query[...], query_inv, query_gain[...])
    grad_qkv[0] = result.astype(jnp.bfloat16)
    incoming = turn_back(grad_key_sum[...] * factor, cosine[...], sine[...])
    result, key_part = through_norm(incoming, key[...], key_inv, key_gain[...])
    grad_qkv[1] = result.astype(jnp.bfloat16)
    grad_qkv[2] = grad_value_sum[...].astype(jnp.bfloat16)
    result, text_part = through_norm(
        text_key_sum[...] * factor, text_key[...], text_inv, key_gain[...]
    )
    grad_text[0] = result.astype(jnp.bfloat16)
    grad_text[1] = text_value_sum[...].astype(jnp.bfloat16)
    gate_part = jnp.sum(grads * cross_out[...], axis=1, keepdims=True)
    lane = lax.broadcasted_iota(jnp.int32, (head_dim, 128), 1)
    gain_sums[0] = jnp.where(
        lane == 0, query_part, jnp.where(lane == 1, key_part + text_part, gate_part)
    )


def attention_specs(heads, head_dim, rows, text_rows):
    def head_block(part, width):
        return pl.BlockSpec((head_dim, width), lambda h, part=part: (part * heads + h, 0))
    def whole(shape):
        return pl.BlockSpec(shape, lambda h: (0,) * len(shape))
    return [
        pl.BlockSpec(memory_space=pltpu.SMEM),
        head_block(0, rows), head_block(1, rows), head_block(2, rows),
        head_block(0, text_rows), head_block(1, text_rows),
        whole((2, 16, rows)), whole((16, text_rows)),
        whole((head_dim // 2, rows)), whole((head_dim // 2, rows)),
        whole((head_dim, 1)), whole((head_dim, 1)),
    ]


def attention_forward(shared, heads, head_dim, clips):
    qkv, text = shared[1], shared[4]
    rows = qkv.shape[1]; text_rows = text.shape[1]
    cols = heads * head_dim
    out = lambda dt: jax.ShapeDtypeStruct((cols, rows), dt)
    hb = pl.BlockSpec((head_dim, rows), lambda h: (h, 0))
    stat = pl.BlockSpec((1, 1, rows), lambda h: (h, 0, 0))
    return pl.pallas_call(
        functools.partial(attend_forward, clips, text_rows // clips),
        grid=(heads,),
        in_specs=attention_specs(heads, head_dim, rows, text_rows),
        out_specs=[hb, hb, hb, stat, stat],
        out_shape=[out(jnp.bfloat16), out(jnp.float32), out(jnp.float32)]
        + [jax.ShapeDtypeStruct((heads, 1, rows), jnp.float32)] * 2,
        compiler_params=pltpu.CompilerParams(vmem_limit_bytes=48 << 20),
        cost_estimate=pl.CostEstimate(flops=4*cols*rows*rows*2, bytes_accessed=cols*rows*24, transcendentals=heads*rows*rows),
    )(*shared)


def attention_backward(shared, grad, kept, heads, head_dim, clips):
    qkv, text = shared[1], shared[4]
    rows = qkv.shape[1]; text_rows = text.shape[1]
    cols = heads * head_dim
    hb = pl.BlockSpec((head_dim, rows), lambda h: (h, 0))
    stat = pl.BlockSpec((1, 1, rows), lambda h: (h, 0, 0))
    return pl.pallas_call(
        functools.partial(attend_backward, clips, text_rows // clips),
        grid=(heads,),
        in_specs=attention_specs(heads, head_dim, rows, text_rows) + [hb, hb, hb, stat, stat],
        out_specs=[
            pl.BlockSpec((3, head_dim, rows), lambda h: (0, h, 0)),
            pl.BlockSpec((2, head_dim, text_rows), lambda h: (0, h, 0)),
            pl.BlockSpec((1, head_dim, 128), lambda h: (h, 0, 0)),
        ],
        out_shape=[
            jax.ShapeDtypeStruct((3, cols, rows), jnp.bfloat16),
            jax.ShapeDtypeStruct((2, cols, text_rows), jnp.bfloat16),
            jax.ShapeDtypeStruct((heads, head_dim, 128), jnp.float32),
        ],
        scratch_shapes=[pltpu.VMEM((head_dim, rows), jnp.float32)] * 3
        + [pltpu.VMEM((head_dim, text_rows), jnp.float32)] * 2,
        compiler_params=pltpu.CompilerParams(vmem_limit_bytes=48 << 20),
        cost_estimate=pl.CostEstimate(flops=10*cols*rows*rows*2, bytes_accessed=cols*rows*30, transcendentals=heads*rows*rows),
    )(*shared, grad, *kept)


def clip_tables(clip_ids, text_lengths, clips, slots):
    rows = clip_ids.shape[0]
    feature = jnp.arange(16, dtype=jnp.int32)[:, None]
    member = feature == clip_ids[None, :]
    query_part = jnp.where(feature < clips, jnp.where(member, 0.0, -apart), jnp.where(feature == clips, -apart, 0.0))
    key_part = member.astype(jnp.float32)
    owner = jnp.repeat(jnp.arange(clips, dtype=jnp.int32), slots)
    slot = jnp.tile(jnp.arange(slots, dtype=jnp.int32), clips)
    dead = slot >= jnp.repeat(text_lengths, slots)
    text_part = jnp.where(feature == clips, dead[None, :], feature == owner[None, :]).astype(jnp.float32)
    return jnp.stack([query_part, key_part]), text_part


def rotary_tables(positions, head_dim):
    half = head_dim // 2
    frequency = jnp.exp(-math.log(10000.0) * jnp.arange(half, dtype=jnp.float32) * 2.0 / head_dim)
    angles = frequency[:, None] * positions.astype(jnp.float32)[None, :]
    return jnp.cos(angles), jnp.sin(angles)


def on_device(
    tokens,
    clip_ids,
    positions,
    timesteps,
    text_states,
    text_lengths,
    out_grad,
    attn_gain,
    ffn_gain,
    query_gain,
    key_gain,
    cross_gate,
    w_query,
    w_key,
    w_value,
    w_out,
    w_text_key,
    w_text_value,
    w_ada,
    w_gate,
    w_up,
    w_down,
):
    tensor_size = lax.axis_size("tensor")
    my_rank = lax.axis_index("tensor")
    local_rows = tokens.shape[0]
    group_rows = local_rows * tensor_size
    model_width = tokens.shape[1]
    head_dim = query_gain.shape[0]
    local_heads = w_query.shape[1] // head_dim
    head_cols = local_heads * head_dim
    clip_count = timesteps.shape[0]
    text_len = text_states.shape[1]
    text_rows = clip_count * text_len
    highest_precision = lax.Precision.HIGHEST
    def my_rows(values):
        return lax.dynamic_slice_in_dim(values, my_rank * local_rows, local_rows)

    tokens_all = lax.all_gather(tokens, "tensor", axis=0, tiled=True)
    group_table = clip_table(clip_ids, clip_count)
    my_table = my_rows(group_table)
    embedded = time_embed(timesteps, w_ada.shape[0])
    condition = (embedded * jax.nn.sigmoid(embedded)).astype(jnp.bfloat16)
    mod_part = jnp.dot(condition, w_ada, preferred_element_type=jnp.float32)
    modulation = lax.all_gather(mod_part, "tensor", axis=1, tiled=True)
    per_token = jnp.dot(my_table, modulation[:, model_width:], precision=highest_precision)
    gate_attn = jnp.tanh(per_token[:, :model_width])
    scale_ffn = per_token[:, model_width : 2 * model_width]
    gate_ffn = jnp.tanh(per_token[:, 2 * model_width :])
    grad_output = out_grad.astype(jnp.float32)
    grad_ffn_low = (grad_output * gate_ffn).astype(jnp.bfloat16)
    grad_ffn_all = lax.all_gather(grad_ffn_low, "tensor", axis=0, tiled=True)
    scale_clips = modulation[:, :model_width]
    scale_all = jnp.dot(group_table, scale_clips, precision=highest_precision)
    inputs_all = tokens_all.astype(jnp.float32)
    normed_all = inputs_all * rms_scale(inputs_all)
    attn_all = (normed_all * attn_gain * (1.0 + scale_all)).astype(jnp.bfloat16)
    inputs = tokens.astype(jnp.float32)
    inv_first = rms_scale(inputs)
    normed_first = inputs * inv_first
    scale_attn = my_rows(scale_all)
    w_qkv = jnp.concatenate([w_query, w_key, w_value], axis=1)
    qkv = product(w_qkv, attn_all, ((0,), (1,)))
    text_flat = text_states.reshape(text_rows, text_states.shape[2])
    text_pair = jnp.concatenate(
        [product(w_text_key, text_flat, ((0,), (1,))), product(w_text_value, text_flat, ((0,), (1,)))],
        axis=0,
    )
    gate_tanh = jnp.tanh(lax.dynamic_slice_in_dim(cross_gate, my_rank * local_heads, local_heads))
    table, text_table = clip_tables(clip_ids, text_lengths, clip_count, text_len)
    cosine, sine = rotary_tables(positions, head_dim)
    shared = (
        gate_tanh, qkv, qkv, qkv, text_pair, text_pair, table, text_table, cosine, sine,
        query_gain[:, None], key_gain[:, None],
    )
    mixed_heads, *kept = attention_forward(shared, local_heads, head_dim, clip_count)
    attn_out = scatter_rows(product(mixed_heads, w_out, ((0,), (0,))))
    middle = inputs + gate_attn * attn_out
    inv_second = rms_scale(middle)
    normed_second = middle * inv_second
    ffn_rows = (normed_second * ffn_gain * (1.0 + scale_ffn)).astype(jnp.bfloat16)
    ffn_all = lax.all_gather(ffn_rows, "tensor", axis=0, tiled=True)
    w_pair = jnp.concatenate([w_gate, w_up], axis=1)
    hidden_cols = w_gate.shape[1]
    pair_pre = jnp.dot(ffn_all, w_pair, preferred_element_type=jnp.float32)
    gate_pre = pair_pre[:, :hidden_cols]
    up_pre = pair_pre[:, hidden_cols:]
    sigmoid_gate = jax.nn.sigmoid(gate_pre)
    silu_gate = gate_pre * sigmoid_gate
    hidden = (silu_gate * up_pre).astype(jnp.bfloat16)
    grad_hidden = jnp.dot(grad_ffn_all, w_down.T, preferred_element_type=jnp.float32)
    grad_gate_low = (
        grad_hidden * up_pre * sigmoid_gate * (1.0 + gate_pre * (1.0 - sigmoid_gate))
    ).astype(jnp.bfloat16)
    grad_up_low = (grad_hidden * silu_gate).astype(jnp.bfloat16)
    grad_pair = jnp.concatenate([grad_gate_low, grad_up_low], axis=1)
    grad_ffn_rows = scatter_rows(jnp.dot(grad_pair, w_pair.T, preferred_element_type=jnp.float32))
    down_sum = scatter_groups(
        jnp.dot(grad_ffn_all.T, hidden, preferred_element_type=jnp.float32).astype(jnp.bfloat16)
    )
    pair_sum = scatter_groups(
        jnp.dot(ffn_all.T, grad_pair, preferred_element_type=jnp.float32).astype(jnp.bfloat16)
    )
    ffn_out = scatter_rows(jnp.dot(hidden, w_down, preferred_element_type=jnp.float32))
    block_out = (middle + gate_ffn * ffn_out).astype(jnp.bfloat16)
    grad_gate_ffn = grad_output * ffn_out * (1.0 - gate_ffn * gate_ffn)
    ffn_gain_part = jnp.sum(grad_ffn_rows * normed_second * (1.0 + scale_ffn), axis=0)
    grad_scale_ffn = grad_ffn_rows * normed_second * ffn_gain
    grad_middle = grad_output + rms_backward(
        grad_ffn_rows * ffn_gain * (1.0 + scale_ffn), normed_second, inv_second
    )
    grad_attn_low = (grad_middle * gate_attn).astype(jnp.bfloat16)
    grad_gate_attn = grad_middle * attn_out * (1.0 - gate_attn * gate_attn)
    grad_attn_all = lax.all_gather(grad_attn_low, "tensor", axis=0, tiled=True)
    out_sum = scatter_groups(
        product(grad_attn_all, mixed_heads, ((0,), (1,))).astype(jnp.bfloat16)
    )
    grad_heads = product(w_out, grad_attn_all, ((1,), (1,))).astype(jnp.bfloat16)
    grad_qkv, grad_text, gain_sums = attention_backward(
        shared, grad_heads, kept, local_heads, head_dim, clip_count
    )
    grad_qkv = grad_qkv.reshape(3 * head_cols, group_rows)
    grad_text = grad_text.reshape(2 * head_cols, text_rows)
    query_gain_part = jnp.sum(gain_sums[:, :, 0], axis=0)
    key_gain_part = jnp.sum(gain_sums[:, :, 1], axis=0)
    grad_cross = jnp.sum(gain_sums[:, :, 2], axis=1) * (1.0 - gate_tanh * gate_tanh)
    rows_part = product(grad_qkv, w_qkv, ((0,), (1,)))
    grad_attn_rows = scatter_rows(rows_part)
    text_sum = scatter_groups(
        product(text_flat, grad_text, ((0,), (1,))).astype(jnp.bfloat16)
    )
    qkv_sum = scatter_groups(
        product(attn_all, grad_qkv, ((0,), (1,))).astype(jnp.bfloat16)
    )
    scaled_part = jnp.dot(group_table.T, rows_part * normed_all, precision=highest_precision)
    attn_gain_part = jnp.sum(scaled_part * (1.0 + scale_clips), axis=0)
    own_mod_grad = jnp.dot(
        my_table.T,
        jnp.concatenate([grad_gate_attn, grad_scale_ffn, grad_gate_ffn], axis=1),
        precision=highest_precision,
    )
    clip_mod_grad = jnp.concatenate([scaled_part * attn_gain, own_mod_grad], axis=1)
    part_cols = mod_part.shape[1]

    def mod_block(rank):
        return lax.dynamic_slice_in_dim(clip_mod_grad, (rank % tensor_size) * part_cols, part_cols, 1)

    mod_grad = mod_block(my_rank)
    for shift in range(1, tensor_size):
        mod_grad = mod_grad + lax.ppermute(
            mod_block(my_rank + shift),
            "tensor",
            [(i, (i + shift) % tensor_size) for i in range(tensor_size)],
        )
    mod_grad_groups = spread_groups(mod_grad.astype(jnp.bfloat16))
    mod_grad_groups = mod_grad_groups.reshape(-1, part_cols)
    condition_groups = spread_groups(condition).reshape(-1, condition.shape[1])
    ada_rows = condition.shape[1] // lax.axis_size("dp")
    my_condition = lax.dynamic_slice_in_dim(
        condition_groups, lax.axis_index("dp") * ada_rows, ada_rows, 1
    )
    ada_sum = jnp.dot(my_condition.T, mod_grad_groups, preferred_element_type=jnp.float32)
    gate_full = lax.dynamic_update_slice_in_dim(
        jnp.zeros((cross_gate.shape[0],), jnp.float32), grad_cross, my_rank * local_heads, 0
    )
    small_parts = (attn_gain_part, ffn_gain_part, query_gain_part, key_gain_part, gate_full)
    small_sum = butterfly_sum(jnp.concatenate(small_parts))
    small_sums = []
    start = 0
    for part in small_parts:
        small_sums.append(small_sum[start : start + part.shape[0]])
        start += part.shape[0]
    input_grad = grad_middle + rms_backward(
        grad_attn_rows * attn_gain * (1.0 + scale_attn), normed_first, inv_first
    )
    return (
        block_out,
        input_grad,
        *small_sums,
        qkv_sum[:, :head_cols],
        qkv_sum[:, head_cols : 2 * head_cols],
        qkv_sum[:, 2 * head_cols :],
        out_sum.T,
        text_sum[:, :head_cols],
        text_sum[:, head_cols:],
        ada_sum,
        pair_sum[:, :hidden_cols],
        pair_sum[:, hidden_cols:],
        down_sum.T,
    )


def solution(mesh):
    return jax.shard_map(
        on_device,
        mesh=mesh,
        in_specs=(
            P(("dp", "tensor"), None),
            P("dp"),
            P("dp"),
            P("dp"),
            P("dp", None, None),
            P("dp"),
            P(("dp", "tensor"), None),
            P(),
            P(),
            P(),
            P(),
            P(),
            P(None, "tensor"),
            P(None, "tensor"),
            P(None, "tensor"),
            P("tensor", None),
            P(None, "tensor"),
            P(None, "tensor"),
            P(None, "tensor"),
            P(None, "tensor"),
            P(None, "tensor"),
            P("tensor", None),
        ),
        out_specs=(
            P(("dp", "tensor"), None),
            P(("dp", "tensor"), None),
            P(),
            P(),
            P(),
            P(),
            P(),
            P("dp", "tensor"),
            P("dp", "tensor"),
            P("dp", "tensor"),
            P("tensor", "dp"),
            P("dp", "tensor"),
            P("dp", "tensor"),
            P("dp", "tensor"),
            P("dp", "tensor"),
            P("dp", "tensor"),
            P("tensor", "dp"),
        ),
        check_vma=False,
    )
```

```python
import functools
import math

import jax
import jax.numpy as jnp
from jax import lax
from jax.experimental import pallas as pl
from jax.experimental.pallas import tpu as pltpu
from jax.sharding import PartitionSpec as P

epsilon = 1e-06


def rms_scale(values):
    return lax.rsqrt(jnp.mean(values * values, axis=-1, keepdims=True) + epsilon)


def rms_backward(grad_hat, normed, scaling):
    return scaling * (grad_hat - normed * jnp.mean(grad_hat * normed, axis=-1, keepdims=True))


def time_embed(time_steps, embed_width):
    half_width = embed_width // 2
    frequency = jnp.exp(-math.log(10000.0) * jnp.arange(half_width, dtype=jnp.float32) / half_width)
    angles = time_steps.astype(jnp.float32)[:, None] * frequency[None, :]
    return jnp.concatenate([jnp.cos(angles), jnp.sin(angles)], axis=-1)


def time_columns(time_steps, first, width, embed_width):
    half_width = embed_width // 2
    columns = first + jnp.arange(width, dtype=jnp.int32)
    frequency = jnp.exp(
        -math.log(10000.0) * (columns % half_width).astype(jnp.float32) / half_width
    )
    angles = time_steps[:, None] * frequency[None, :]
    embedded = jnp.where((columns < half_width)[None, :], jnp.cos(angles), jnp.sin(angles))
    return (embedded * jax.nn.sigmoid(embedded)).astype(jnp.bfloat16)


def exchange(values, axis_name, distance):
    count = lax.axis_size(axis_name)
    return lax.ppermute(values, axis_name, [(i, i ^ distance) for i in range(count)])


def product(left, right, contract=((1,), (0,))):
    return lax.dot_general(left, right, (contract, ((), ())), preferred_element_type=jnp.float32)


def head_norm(raw):
    return lax.rsqrt(jnp.mean(raw * raw, axis=0, keepdims=True) + epsilon)


def turn(values, cosine, sine):
    half = values.shape[0] // 2
    lead, tail = values[:half], values[half:]
    return jnp.concatenate([lead * cosine - tail * sine, lead * sine + tail * cosine], axis=0)


def turn_back(values, cosine, sine):
    half = values.shape[0] // 2
    lead, tail = values[:half], values[half:]
    return jnp.concatenate([lead * cosine + tail * sine, tail * cosine - lead * sine], axis=0)


def widen(values, extra):
    rows = values.shape[0] + extra.shape[0]
    pad = jnp.zeros((128 - rows, values.shape[1]), values.dtype)
    return jnp.concatenate([values, extra.astype(values.dtype), pad], axis=0)


def text_range(block, blocks, clips, slots):
    first = 0 if block == 0 else slots
    last = (clips if block == blocks - 1 else clips - 1) * slots
    return first, last


def total(terms):
    result = terms[0].astype(jnp.float32)
    for term in terms[1:]:
        result = result + term.astype(jnp.float32)
    return result


edge_rows = 256
apart = 2048.0
vmem_bytes = 56 << 20


def params():
    return pltpu.CompilerParams(vmem_limit_bytes=vmem_bytes)


def costs(flops, moved, transcendentals=0):
    return pl.CostEstimate(flops=flops // 64, bytes_accessed=moved // 64, transcendentals=0)


def struct(shape, kind=jnp.float32):
    return jax.ShapeDtypeStruct(shape, kind)


smem_spec = pl.BlockSpec(memory_space=pltpu.SMEM)


def whole_spec(shape):
    return pl.BlockSpec(shape, lambda *at: (0,) * len(shape))


def modulation_rows(mod, rank, which):
    count = mod.shape[0]
    per = count // 4
    shares = [mod[lax.rem(which * per + i - rank + count, count)] for i in range(per)]
    return shares[0] if per == 1 else jnp.concatenate(shares, axis=1)


def by_clip(vectors, ids):
    result = vectors[0:1]
    for clip in range(1, vectors.shape[0]):
        result = jnp.where(ids == clip, vectors[clip : clip + 1], result)
    return result


def sums_by_clip(values, ids, clips):
    return jnp.concatenate(
        [
            jnp.sum(jnp.where(ids == clip, values, 0.0), axis=0, keepdims=True)
            for clip in range(clips)
        ],
        axis=0,
    )


def gate_kernel(rank, mod, ids, out_grad, result):
    gate = by_clip(jnp.tanh(modulation_rows(mod, rank[0], 3)), ids[...])
    result[...] = (out_grad[...].astype(jnp.float32) * gate).astype(jnp.bfloat16)


def gated_gradient(rank, mod, ids, out_grad):
    return pl.pallas_call(
        gate_kernel,
        in_specs=[smem_spec] + [pl.BlockSpec(memory_space=pltpu.VMEM)] * 3,
        out_shape=struct(out_grad.shape, jnp.bfloat16),
        compiler_params=params(),
        cost_estimate=costs(out_grad.size * 4, out_grad.size * 4),
    )(rank, mod, ids, out_grad)


def project_kernel(rank, mod, ids, gain, tokens, w_query, w_key, w_value, rows_out, qkv):
    inputs = tokens[...].astype(jnp.float32)
    scaled = gain[...] * (1.0 + modulation_rows(mod, rank[0], 0))
    rows = (inputs * rms_scale(inputs) * by_clip(scaled, ids[...])).astype(jnp.bfloat16)
    rows_out[...] = rows
    for part, weight in enumerate((w_query, w_key, w_value)):
        qkv[part] = product(rows, weight[...]).T


def project(rank, mod, ids, gain, tokens_all, w_query, w_key, w_value):
    rows, width = tokens_all.shape
    cols = w_query.shape[1]
    step = edge_rows
    return pl.pallas_call(
        project_kernel,
        grid=(rows // step,),
        in_specs=[
            smem_spec, whole_spec(mod.shape), pl.BlockSpec((step, 1), lambda i: (i, 0)),
            whole_spec(gain.shape), pl.BlockSpec((step, width), lambda i: (i, 0)),
            whole_spec((width, cols)), whole_spec((width, cols)), whole_spec((width, cols)),
        ],
        out_specs=[
            pl.BlockSpec((step, width), lambda i: (i, 0)),
            pl.BlockSpec((3, cols, step), lambda i: (0, 0, i)),
        ],
        out_shape=[struct((rows, width), jnp.bfloat16), struct((3, cols, rows))],
        compiler_params=params(),
        cost_estimate=costs(6 * rows * width * cols, rows * width * 4 + 3 * cols * (width * 2 + rows * 4)),
    )(rank, mod, ids, gain, tokens_all, w_query, w_key, w_value)


def assemble_kernel(mine, held, arrived, out):
    core = mine[0] & 1
    out[:, core] = held[0]
    out[:, 1 - core] = arrived[0]


def assemble(held, arrived):
    half, ranks, rows, width = held.shape
    bits = half.bit_length() - 1

    def place(i, mine):
        pair = sum(((i >> k) & 1) << (bits - 1 - k) for k in range(bits))
        return 0, (mine[0] >> 1) ^ pair, 0, 0

    spec = pl.BlockSpec((1, ranks, rows, width), lambda i, mine: (i, 0, 0, 0))
    return pl.pallas_call(
        assemble_kernel,
        grid_spec=pltpu.PrefetchScalarGridSpec(
            num_scalar_prefetch=1,
            grid=(half,),
            in_specs=[spec, spec],
            out_specs=pl.BlockSpec((ranks, 2, rows, width), place),
        ),
        out_shape=struct((ranks, 2 * half, rows, width), held.dtype),
        compiler_params=params(),
        cost_estimate=costs(0, 0),
    )(lax.axis_index("dp")[None], held, arrived)


def middle_kernel(count, rank, mod, ids, gain, tokens, w_out, *refs):
    mixed, (attn_out, middle, *rows_out) = refs[:count], refs[count:]
    total = product(mixed[0][...], w_out[0], ((0,), (0,)))
    for m in range(1, count):
        total += product(mixed[m][...], w_out[m], ((0,), (0,)))
    attn_out[...] = total
    where_clip = ids[...]
    gate = by_clip(jnp.tanh(modulation_rows(mod, rank[0], 1)), where_clip)
    values = tokens[...].astype(jnp.float32) + gate * total
    middle[...] = values
    scaled = gain[...] * (1.0 + modulation_rows(mod, rank[0], 2))
    rows = (values * rms_scale(values) * by_clip(scaled, where_clip)).astype(jnp.bfloat16)
    step = rows.shape[0] // len(rows_out)
    for cut, ref in enumerate(rows_out):
        ref[...] = rows[cut * step : (cut + 1) * step]


def middle_forward(rank, mod, ids, gain, tokens, w_out_all, mixed, cuts):
    rows, width = tokens.shape
    vmem = pl.BlockSpec(memory_space=pltpu.VMEM)
    return pl.pallas_call(
        functools.partial(middle_kernel, len(mixed)),
        in_specs=[smem_spec] + [vmem] * (5 + len(mixed)),
        out_shape=[struct((rows, width))] * 2
        + [struct((rows // cuts, width), jnp.bfloat16)] * cuts,
        compiler_params=params(),
        cost_estimate=costs(2 * rows * w_out_all.size // 1, w_out_all.size * 2 + rows * width * 14),
    )(rank, mod, ids, gain, tokens, w_out_all, *mixed)


def middle_back_kernel(cuts, count, rank, mod, ids, gain, middle, attn_out, out_grad, w_out, *refs):
    pieces = []
    at = 0
    for terms in cuts:
        pieces.append(total([ref[...] for ref in refs[at : at + terms]]))
        at += terms
    grad_middle, grad_low, scale_sums, gate_sums = refs[at : at + 4]
    grad_mixed = refs[at + 4 :]
    clips = mod.shape[1]
    where_clip = ids[...]
    values = middle[...]
    inverse = rms_scale(values)
    normed = values * inverse
    grads = jnp.concatenate(pieces, axis=0)
    scale_sums[...] = sums_by_clip(grads * normed, where_clip, clips)
    scaled = gain[...] * (1.0 + modulation_rows(mod, rank[0], 2))
    result = out_grad[...].astype(jnp.float32) + rms_backward(
        grads * by_clip(scaled, where_clip), normed, inverse
    )
    grad_middle[...] = result
    gate = jnp.tanh(modulation_rows(mod, rank[0], 1))
    gate_sums[...] = sums_by_clip(result * attn_out[...], where_clip, clips)
    low = (result * by_clip(gate, where_clip)).astype(jnp.bfloat16)
    grad_low[...] = low
    for m in range(count):
        grad_mixed[m][...] = product(w_out[m], low, ((1,), (1,))).astype(jnp.bfloat16)


def middle_backward(rank, mod, ids, gain, middle, attn_out, out_grad, w_out_all, pieces):
    rows, width = middle.shape
    count, cols, _ = w_out_all.shape
    clips = mod.shape[1]
    vmem = pl.BlockSpec(memory_space=pltpu.VMEM)
    return pl.pallas_call(
        functools.partial(middle_back_kernel, [len(terms) for terms in pieces], count),
        in_specs=[smem_spec] + [vmem] * (7 + sum(len(terms) for terms in pieces)),
        out_shape=[
            struct((rows, width)), struct((rows, width), jnp.bfloat16),
            struct((clips, width)), struct((clips, width)),
        ]
        + [struct((cols, rows), jnp.bfloat16)] * count,
        compiler_params=params(),
        cost_estimate=costs(2 * rows * w_out_all.size, w_out_all.size * 2 + rows * width * 20),
    )(rank, mod, ids, gain, middle, attn_out, out_grad, w_out_all, *sum(pieces, []))


def ffn_kernel(rows, grads, w_gate, w_up, w_down, hidden, grad_gate, grad_up, back, out):
    gate_pre = product(rows[...], w_gate[...])
    up_pre = product(rows[...], w_up[...])
    grad_hidden = product(grads[...], w_down[...], ((1,), (1,)))
    sigmoid = 1.0 / (1.0 + jnp.exp(-gate_pre))
    silu = gate_pre * sigmoid
    hidden_low = (silu * up_pre).astype(jnp.bfloat16)
    gate_low = (grad_hidden * up_pre * (sigmoid + silu * (1.0 - sigmoid))).astype(jnp.bfloat16)
    up_low = (grad_hidden * silu).astype(jnp.bfloat16)
    hidden[...] = hidden_low
    grad_gate[...] = gate_low
    grad_up[...] = up_low
    back[...] = (
        product(gate_low, w_gate[...], ((1,), (1,))) + product(up_low, w_up[...], ((1,), (1,)))
    ).astype(jnp.bfloat16)
    out[...] = product(hidden_low, w_down[...]).astype(jnp.bfloat16)


def feed_forward(rows, grads, w_gate, w_up, w_down):
    count, width = rows.shape
    hidden = w_gate.shape[1]
    step = edge_rows
    wide = pl.BlockSpec((step, width), lambda i: (i, 0))
    inner = pl.BlockSpec((step, hidden), lambda i: (i, 0))
    return pl.pallas_call(
        ffn_kernel,
        grid=(count // step,),
        in_specs=[
            wide, wide, whole_spec(w_gate.shape), whole_spec(w_up.shape), whole_spec(w_down.shape),
        ],
        out_specs=[inner] * 3 + [wide] * 2,
        out_shape=[struct((count, hidden), jnp.bfloat16)] * 3
        + [struct((count, width), jnp.bfloat16)] * 2,
        compiler_params=params(),
        cost_estimate=costs(12 * count * width * hidden, 6 * width * hidden + 8 * count * width, count * hidden),
    )(rows, grads, w_gate, w_up, w_down)


def input_kernel(ids, tokens, grad_qkv, w_query, w_key, w_value, result, sums):
    clips = sums.shape[0]
    total = None
    for part, weight in enumerate((w_query, w_key, w_value)):
        term = lax.dot_general(
            grad_qkv[part], weight[...], (((0,), (1,)), ((), ())), preferred_element_type=jnp.float32
        )
        total = term if total is None else total + term
    result[...] = total.astype(jnp.bfloat16)
    inputs = tokens[...].astype(jnp.float32)
    found = sums_by_clip(total * (inputs * rms_scale(inputs)), ids[...], clips)

    @pl.when(pl.program_id(0) == 0)
    def _():
        sums[...] = found

    @pl.when(pl.program_id(0) > 0)
    def _():
        sums[...] += found


def input_rows(ids, tokens_all, grad_qkv, w_query, w_key, w_value, clips):
    rows, width = tokens_all.shape
    cols = w_query.shape[1]
    step = edge_rows
    return pl.pallas_call(
        input_kernel,
        grid=(rows // step,),
        in_specs=[
            pl.BlockSpec((step, 1), lambda i: (i, 0)), pl.BlockSpec((step, width), lambda i: (i, 0)),
            pl.BlockSpec((3, cols, step), lambda i: (0, 0, i)),
            whole_spec((width, cols)), whole_spec((width, cols)), whole_spec((width, cols)),
        ],
        out_specs=[pl.BlockSpec((step, width), lambda i: (i, 0)), whole_spec((clips, width))],
        out_shape=[struct((rows, width), jnp.bfloat16), struct((clips, width))],
        compiler_params=params(),
        cost_estimate=costs(6 * rows * width * cols, rows * width * 4 + 6 * cols * (width + rows)),
    )(ids, tokens_all, grad_qkv, w_query, w_key, w_value)


def block_kernel(cuts, rank, mod, ids, middle, out_grad, *refs):
    block_out, sums = refs[cuts:]
    where_clip = ids[...]
    ffn_out = jnp.concatenate([ref[...] for ref in refs[:cuts]], axis=0).astype(jnp.float32)
    gate = by_clip(jnp.tanh(modulation_rows(mod, rank[0], 3)), where_clip)
    block_out[...] = (middle[...] + gate * ffn_out).astype(jnp.bfloat16)
    sums[...] = sums_by_clip(out_grad[...].astype(jnp.float32) * ffn_out, where_clip, mod.shape[1])


def block_result(rank, mod, ids, middle, out_grad, pieces):
    vmem = pl.BlockSpec(memory_space=pltpu.VMEM)
    return pl.pallas_call(
        functools.partial(block_kernel, len(pieces)),
        in_specs=[smem_spec] + [vmem] * (4 + len(pieces)),
        out_shape=[struct(middle.shape, jnp.bfloat16), struct((mod.shape[1], middle.shape[1]))],
        compiler_params=params(),
        cost_estimate=costs(middle.size * 8, middle.size * 10),
    )(rank, mod, ids, middle, out_grad, *pieces)


def last_kernel(rank, mod, ids, gain, tokens, grad_middle, grads, result):
    inputs = tokens[...].astype(jnp.float32)
    inverse = rms_scale(inputs)
    scaled = by_clip(gain[...] * (1.0 + modulation_rows(mod, rank[0], 0)), ids[...])
    result[...] = grad_middle[...] + rms_backward(
        grads[...].astype(jnp.float32) * scaled, inputs * inverse, inverse
    )


def input_result(rank, mod, ids, gain, tokens, grad_middle, grads):
    vmem = pl.BlockSpec(memory_space=pltpu.VMEM)
    return pl.pallas_call(
        last_kernel,
        in_specs=[smem_spec] + [vmem] * 6,
        out_shape=struct(tokens.shape),
        compiler_params=params(),
        cost_estimate=costs(tokens.size * 12, tokens.size * 12),
    )(rank, mod, ids, gain, tokens, grad_middle, grads)


def weight_kernel(lefts, rights, block, mine, *refs):
    left = refs[: len(lefts)]
    right = refs[len(lefts) : len(lefts) + sum(rights)]
    given, kept, left_turned, whole = refs[-4:]
    step = pl.program_id(0)

    @pl.when(step == 0)
    def _():
        at = 0
        for ref, relative in zip(left, lefts):
            if relative:
                count = ref.shape[0]
                places = [lax.rem(mine[1] + m, count) for m in range(count)]
                values = jnp.concatenate([ref[place, 0] for place in places], axis=0)
            else:
                values = ref[...]
                values = values.reshape(-1, values.shape[-1])
            left_turned[:, at : at + values.shape[0]] = values.T
            at += values.shape[0]

    tiles = pl.num_programs(0) // len(rights)
    first = 0
    for share, count in enumerate(rights):
        chosen = right[first : first + count]
        first += count

        @pl.when(step // tiles == share)
        def _(chosen=chosen):
            at = 0
            result = None
            for ref in chosen:
                values = ref[...]
                term = product(left_turned[:, at : at + values.shape[0]], values)
                result = term if result is None else result + term
                at += values.shape[0]
            whole[...] = result.astype(jnp.bfloat16)

    for pair in range(given.shape[0]):
        for ref, side in ((given, 1 - mine[0]), (kept, mine[0])):
            start = pl.multiple_of((2 * pair + side) * block, 16)
            ref[pair] = whole[pl.ds(start, block)]


def weight_gradient(lefts, left_specs, relative, rights, depth, width, columns, tile, place, before):
    count = lax.axis_size("dp")
    mine = jnp.stack([lax.axis_index("dp") & 1, lax.axis_index("tensor")])
    block = width // count
    tiles = rights[0][0].shape[1] // tile
    out_spec = pl.BlockSpec((count // 2, block, tile), lambda i: (0, 0, place(i)))
    right_specs = [
        pl.BlockSpec(
            (ref.shape[0], tile), lambda i, share=share: (0, jnp.clip(i - share * tiles, 0, tiles - 1))
        )
        for share, refs in enumerate(rights)
        for ref in refs
    ]
    operands = [mine, *lefts, *sum(rights, []), *before]
    first = len(operands) - len(before)
    return pl.pallas_call(
        functools.partial(weight_kernel, relative, [len(refs) for refs in rights], block),
        grid=(tiles * len(rights),),
        in_specs=[smem_spec]
        + left_specs
        + right_specs
        + [pl.BlockSpec(memory_space=pl.ANY)] * len(before),
        out_specs=[out_spec] * 2,
        out_shape=[struct((count // 2, block, columns), jnp.bfloat16)] * 2,
        scratch_shapes=[pltpu.VMEM((width, depth), jnp.bfloat16), pltpu.VMEM((width, tile), jnp.bfloat16)],
        input_output_aliases={first + k: k for k in range(len(before))},
        compiler_params=params(),
        cost_estimate=costs(2 * depth * width * columns, 2 * (depth + columns) * (width + depth)),
    )(*operands)


def text_kernel(places, grads, first, second, out):
    half = grads.shape[1]
    out[0] = product(grads[0], first[...]).astype(jnp.bfloat16)
    out[1] = product(grads[1], second[...]).astype(jnp.bfloat16)


def text_gradient(grads, text_flat, side):
    count = lax.axis_size("dp")
    mine = lax.axis_index("dp")
    bits = count.bit_length() - 1
    length = text_flat.shape[1] // count
    half = count // 2
    places = []
    for order in bit_orders():
        for place in range(half):
            j = side + sum(
                1 << bit for at, bit in enumerate(order[1:]) if (place >> (bits - 2 - at)) & 1
            )
            places.append(mine ^ j)
    places = jnp.stack(places)
    cols = grads.shape[1]
    rows = text_flat.shape[0]
    return pl.pallas_call(
        text_kernel,
        grid_spec=pltpu.PrefetchScalarGridSpec(
            num_scalar_prefetch=1,
            grid=(half,),
            in_specs=[
                pl.BlockSpec(grads.shape, lambda i, at: (0, 0, 0)),
                pl.BlockSpec((rows, length), lambda i, at: (0, at[i])),
                pl.BlockSpec((rows, length), lambda i, at: (0, at[half + i])),
            ],
            out_specs=pl.BlockSpec((2, cols, length), lambda i, at: (0, 0, i)),
        ),
        out_shape=struct((2, cols, half * length), jnp.bfloat16),
        compiler_params=params(),
        cost_estimate=costs(4 * cols * rows * half * length, 4 * rows * half * length),
    )(places, grads, text_flat, text_flat)


def attend_forward(
    clips, slots, ranks, gates, query, key, value, text_key, text_value, table, text_table, cosine, sine,
    query_gain, key_gain, mixed, self_out, cross_out, self_inverse, cross_inverse,
):
    head_dim, rows = query.shape
    scale = math.log2(math.e) / math.sqrt(head_dim)
    gate = gates[pl.program_id(0)]
    raw = query[...]
    query_rot = turn(raw * head_norm(raw) * query_gain[...], cosine[...], sine[...])
    query_wide = widen(query_rot, table[0]).astype(jnp.bfloat16)
    raw = key[...]
    key_rot = turn(raw * head_norm(raw) * key_gain[...], cosine[...], sine[...])
    key_wide = widen(key_rot, table[1]).T.astype(jnp.bfloat16)
    raw = text_key[...]
    text_wide = widen(raw * head_norm(raw) * key_gain[...], text_table[...]).T.astype(jnp.bfloat16)
    ones_row = (lax.broadcasted_iota(jnp.int32, (16, rows), 0) == 0).astype(jnp.float32)
    value_wide = jnp.concatenate([value[...], ones_row], axis=0).astype(jnp.bfloat16)
    text_value_wide = jnp.concatenate(
        [text_value[...], ones_row[:, : text_value.shape[1]]], axis=0
    ).astype(jnp.bfloat16)
    blocks = rows // edge_rows
    for block in range(blocks):
        cols = slice(block * edge_rows, (block + 1) * edge_rows)
        query_blk = query_wide[:, cols]
        weights = jnp.exp2(product(key_wide, query_blk) * scale).astype(jnp.bfloat16)
        total = product(value_wide, weights)
        inverse = 1.0 / total[head_dim : head_dim + 1]
        own = total[:head_dim] * inverse
        first, last = text_range(block, blocks, clips, slots)
        weights = jnp.exp2(product(text_wide[first:last], query_blk) * scale).astype(jnp.bfloat16)
        total = product(text_value_wide[:, first:last], weights)
        text_inverse = 1.0 / total[head_dim : head_dim + 1]
        other = total[:head_dim] * text_inverse
        pieces = mixed.shape[0]
        mixed[lax.rem(block - ranks[0] + pieces, pieces)] = (own + gate * other).astype(jnp.bfloat16)
        self_out[:, cols] = own
        cross_out[:, cols] = other
        self_inverse[0, :, cols] = inverse
        cross_inverse[0, :, cols] = text_inverse


def through_norm(incoming, raw, inverse, gain):
    normed = raw * inverse
    scaled = incoming * gain
    mean = jnp.mean(scaled * normed, axis=0, keepdims=True)
    gain_part = jnp.sum(incoming * normed, axis=1, keepdims=True)
    return inverse * (scaled - normed * mean), gain_part


def rank_pieces(ranks, grads, held):
    count = len(grads)
    for m, ref in enumerate(grads):
        held[m] = ref[...].astype(jnp.float32)
    return jnp.concatenate(
        [held[lax.rem(piece - ranks[0] + count, count)] for piece in range(count)], axis=1
    )


def with_dots(weighted, out):
    rows = out.shape[1]
    low = weighted.astype(jnp.bfloat16)
    dots = jnp.sum(low.astype(jnp.float32) * out, axis=0, keepdims=True)
    high = dots.astype(jnp.bfloat16).astype(jnp.float32)
    rows_at = lax.broadcasted_iota(jnp.int32, (16, rows), 0)
    extra = jnp.where(rows_at == 0, -high, jnp.where(rows_at == 1, high - dots, 0.0))
    return widen(low.astype(jnp.float32), extra).astype(jnp.bfloat16)


def two_ones(rows):
    return (lax.broadcasted_iota(jnp.int32, (16, rows), 0) < 2).astype(jnp.float32)


def cross_backward(
    clips, slots, count, ranks, gates, query, text_key, text_value, table, text_table, cosine, sine,
    query_gain, key_gain, cross_out, cross_inverse, *refs,
):
    grad_pieces = refs[:count]
    grad_text, grad_query, gain_sums, held, text_key_sum, text_value_sum = refs[count:]
    head_dim, rows = query.shape
    scale = math.log2(math.e) / math.sqrt(head_dim)
    factor = 1.0 / math.sqrt(head_dim)
    gate = gates[pl.program_id(0)]
    raw = query[...]
    query_rot = turn(raw * head_norm(raw) * query_gain[...], cosine[...], sine[...])
    query_wide = widen(query_rot, table[0]).astype(jnp.bfloat16)
    raw = text_key[...]
    text_inv = head_norm(raw)
    text_norm = raw * text_inv * key_gain[...]
    text_low = text_norm.astype(jnp.bfloat16)
    text_wide = widen(text_norm, text_table[...]).T.astype(jnp.bfloat16)
    text_value_wide = widen(text_value[...], two_ones(text_value.shape[1])).T.astype(jnp.bfloat16)
    grads = rank_pieces(ranks, grad_pieces, held)
    cross_wide = with_dots(grads * (gate * cross_inverse[0]), cross_out[...])
    blocks = rows // edge_rows
    text_key_sum[...] = jnp.zeros_like(text_key_sum)
    text_value_sum[...] = jnp.zeros_like(text_value_sum)
    for block in range(blocks):
        cols = slice(block * edge_rows, (block + 1) * edge_rows)
        query_blk = query_wide[:, cols]
        first, last = text_range(block, blocks, clips, slots)
        grad_blk = cross_wide[:, cols]
        weights = jnp.exp2(product(text_wide[first:last], query_blk) * scale)
        slopes = (weights * product(text_value_wide[first:last], grad_blk)).astype(jnp.bfloat16)
        text_value_sum[:, first:last] += product(
            grad_blk[:head_dim], weights.astype(jnp.bfloat16), ((1,), (1,))
        )
        text_key_sum[:, first:last] += product(query_blk[:head_dim], slopes, ((1,), (1,)))
        grad_query[:, cols] = product(text_low[:, first:last], slopes)
    result, text_part = through_norm(
        text_key_sum[...] * factor, text_key[...], text_inv, key_gain[...]
    )
    grad_text[0] = result.astype(jnp.bfloat16)
    grad_text[1] = text_value_sum[...].astype(jnp.bfloat16)
    gate_part = jnp.sum(grads * cross_out[...], axis=1, keepdims=True)
    lane = lax.broadcasted_iota(jnp.int32, (head_dim, 128), 1)
    gain_sums[0] = jnp.where(lane == 0, text_part, gate_part)


def self_backward(
    count, ranks, query, key, value, table, cosine, sine, query_gain, key_gain,
    self_out, self_inverse, grad_query, *refs,
):
    grad_pieces = refs[:count]
    grad_qkv, gain_sums, held, grad_key_sum, grad_value_sum, grad_query_all = refs[count:]
    head_dim, rows = query.shape
    scale = math.log2(math.e) / math.sqrt(head_dim)
    factor = 1.0 / math.sqrt(head_dim)
    raw = query[...]
    query_inv = head_norm(raw)
    query_rot = turn(raw * query_inv * query_gain[...], cosine[...], sine[...])
    query_wide = widen(query_rot, table[0]).astype(jnp.bfloat16)
    raw = key[...]
    key_inv = head_norm(raw)
    key_rot = turn(raw * key_inv * key_gain[...], cosine[...], sine[...])
    key_low = key_rot.astype(jnp.bfloat16)
    key_wide = widen(key_rot, table[1]).T.astype(jnp.bfloat16)
    value_wide = widen(value[...], two_ones(rows)).T.astype(jnp.bfloat16)
    self_wide = with_dots(
        rank_pieces(ranks, grad_pieces, held) * self_inverse[0], self_out[...]
    )
    for block in range(rows // edge_rows):
        cols = slice(block * edge_rows, (block + 1) * edge_rows)
        query_blk = query_wide[:, cols]
        grad_blk = self_wide[:, cols]
        weights = jnp.exp2(product(key_wide, query_blk) * scale)
        slopes = (weights * product(value_wide, grad_blk)).astype(jnp.bfloat16)
        value_term = product(grad_blk[:head_dim], weights.astype(jnp.bfloat16), ((1,), (1,)))
        key_term = product(query_blk[:head_dim], slopes, ((1,), (1,)))
        if block == 0:
            grad_value_sum[...] = value_term
            grad_key_sum[...] = key_term
        else:
            grad_value_sum[...] += value_term
            grad_key_sum[...] += key_term
        grad_query_all[:, cols] = grad_query[:, cols] + product(key_low, slopes)

    incoming = turn_back(grad_query_all[...] * factor, cosine[...], sine[...])
    result, query_part = through_norm(incoming, query[...], query_inv, query_gain[...])
    grad_qkv[0] = result.astype(jnp.bfloat16)
    incoming = turn_back(grad_key_sum[...] * factor, cosine[...], sine[...])
    result, key_part = through_norm(incoming, key[...], key_inv, key_gain[...])
    grad_qkv[1] = result.astype(jnp.bfloat16)
    grad_qkv[2] = grad_value_sum[...].astype(jnp.bfloat16)
    lane = lax.broadcasted_iota(jnp.int32, (head_dim, 128), 1)
    gain_sums[0] = jnp.where(lane == 0, query_part, key_part)


def attention_specs(heads, head_dim, rows, text_rows):
    def head_block(part, width):
        return pl.BlockSpec((head_dim, width), lambda h, part=part: (part * heads + h, 0))

    return [
        smem_spec, smem_spec,
        head_block(0, rows), head_block(1, rows), head_block(2, rows),
        head_block(0, text_rows), head_block(0, text_rows),
        whole_spec((2, 16, rows)), whole_spec((16, text_rows)),
        whole_spec((head_dim // 2, rows)), whole_spec((head_dim // 2, rows)),
        whole_spec((head_dim, 1)), whole_spec((head_dim, 1)),
    ]


def attention_forward(shared, heads, head_dim, clips, ranks):
    qkv, text = shared[2], shared[5]
    rows = qkv.shape[1]
    text_rows = text.shape[1]
    cols = heads * head_dim
    hb = pl.BlockSpec((head_dim, rows), lambda h: (h, 0))
    stat = pl.BlockSpec((1, 1, rows), lambda h: (h, 0, 0))
    return pl.pallas_call(
        functools.partial(attend_forward, clips, text_rows // clips),
        grid=(heads,),
        in_specs=attention_specs(heads, head_dim, rows, text_rows),
        out_specs=[
            pl.BlockSpec((ranks, head_dim, rows // ranks), lambda h: (0, h, 0)), hb, hb, stat, stat,
        ],
        out_shape=[struct((ranks, cols, rows // ranks), jnp.bfloat16)]
        + [struct((cols, rows))] * 2
        + [struct((heads, 1, rows))] * 2,
        compiler_params=params(),
        cost_estimate=costs(8 * cols * rows * rows, cols * rows * 24, heads * rows * rows),
    )(*shared)


def attention_backward(shared, grads, kept, heads, head_dim, clips, between):
    (rank, gates, qkv, _, _, text_key, text_value, table, text_table, cosine, sine, query_gain,
     key_gain) = shared
    self_out, cross_out, self_inverse, cross_inverse = kept
    rows = qkv.shape[1]
    text_rows = text_key.shape[1]
    cols = heads * head_dim
    count = len(grads)
    (smem, _, query_s, key_s, value_s, text_key_s, text_value_s, table_s, text_table_s, cos_s,
     sin_s, query_gain_s, key_gain_s) = attention_specs(heads, head_dim, rows, text_rows)
    hb = pl.BlockSpec((head_dim, rows), lambda h: (h, 0))
    stat = pl.BlockSpec((1, 1, rows), lambda h: (h, 0, 0))
    sums = pl.BlockSpec((1, head_dim, 128), lambda h: (h, 0, 0))
    grad_specs = [pl.BlockSpec((head_dim, rows // count), lambda h: (h, 0))] * count
    held = pltpu.VMEM((count, head_dim, rows // count), jnp.float32)
    grad_text, grad_query, cross_sums = pl.pallas_call(
        functools.partial(cross_backward, clips, text_rows // clips, count),
        grid=(heads,),
        in_specs=[
            smem, smem, query_s, text_key_s, text_value_s, table_s, text_table_s, cos_s, sin_s,
            query_gain_s, key_gain_s, hb, stat, *grad_specs,
        ],
        out_specs=[pl.BlockSpec((2, head_dim, text_rows), lambda h: (0, h, 0)), hb, sums],
        out_shape=[
            struct((2, cols, text_rows), jnp.bfloat16), struct((cols, rows)),
            struct((heads, head_dim, 128)),
        ],
        scratch_shapes=[held] + [pltpu.VMEM((head_dim, text_rows), jnp.float32)] * 2,
        compiler_params=params(),
        cost_estimate=costs(6 * cols * rows * text_rows, cols * rows * 14, heads * rows * text_rows // 2),
    )(rank, gates, qkv, text_key, text_value, table, text_table, cosine, sine, query_gain, key_gain,
      cross_out, cross_inverse, *grads)
    grad_query, passed = between(grad_query, grad_text)
    grad_qkv, self_sums = pl.pallas_call(
        functools.partial(self_backward, count),
        grid=(heads,),
        in_specs=[
            smem, query_s, key_s, value_s, table_s, cos_s, sin_s, query_gain_s, key_gain_s,
            hb, stat, hb, *grad_specs,
        ],
        out_specs=[pl.BlockSpec((3, head_dim, rows), lambda h: (0, h, 0)), sums],
        out_shape=[struct((3, cols, rows), jnp.bfloat16), struct((heads, head_dim, 128))],
        scratch_shapes=[held] + [pltpu.VMEM((head_dim, rows), jnp.float32)] * 3,
        compiler_params=params(),
        cost_estimate=costs(20 * cols * rows * rows, cols * rows * 24, heads * rows * rows),
    )(rank, qkv, qkv, qkv, table, cosine, sine, query_gain, key_gain, self_out, self_inverse,
      grad_query, *grads)
    return grad_qkv, grad_text, cross_sums, self_sums, passed


def clip_tables(clip_ids, text_lengths, clips, slots):
    rows = clip_ids.shape[0]
    feature = jnp.arange(16, dtype=jnp.int32)[:, None]
    member = feature == clip_ids[None, :]
    query_part = jnp.where(feature < clips, jnp.where(member, 0.0, -apart), jnp.where(feature == clips, -apart, 0.0))
    key_part = member.astype(jnp.float32)
    owner = jnp.repeat(jnp.arange(clips, dtype=jnp.int32), slots)
    slot = jnp.tile(jnp.arange(slots, dtype=jnp.int32), clips)
    dead = slot >= jnp.repeat(text_lengths, slots)
    text_part = jnp.where(feature == clips, dead[None, :], feature == owner[None, :]).astype(jnp.float32)
    return jnp.stack([query_part, key_part]), text_part


def rotary_tables(positions, head_dim):
    half = head_dim // 2
    frequency = jnp.exp(-math.log(10000.0) * jnp.arange(half, dtype=jnp.float32) * 2.0 / head_dim)
    angles = frequency[:, None] * positions.astype(jnp.float32)[None, :]
    return jnp.cos(angles), jnp.sin(angles)


def sum_kernel(jobs, mine, *refs):
    at = 0
    outs = refs[sum(count for count, _ in jobs) :]
    for (count, turned), out in zip(jobs, outs):
        value = total([ref[0] for ref in refs[at : at + count]])
        value = value.T if turned else value
        if len(out.shape) == 3:
            out[0] = value.astype(out.dtype)
        else:
            out[...] = value.astype(out.dtype)
        at += count


def sum_stage(jobs, steps):
    mine = lax.axis_index("dp")[None]
    terms = [term for job in jobs for term, _ in job[0]]
    return pl.pallas_call(
        functools.partial(sum_kernel, [(len(job[0]), job[3]) for job in jobs]),
        grid_spec=pltpu.PrefetchScalarGridSpec(
            num_scalar_prefetch=1,
            grid=(steps,),
            in_specs=[spec for job in jobs for _, spec in job[0]],
            out_specs=[job[2] for job in jobs],
        ),
        out_shape=[job[1] for job in jobs],
        compiler_params=params(),
        cost_estimate=costs(0, 0),
    )(mine, *terms)


class Scatter:
    def __init__(self, kept, taken, order, column, columns, turned=False):
        bits = lax.axis_size("dp").bit_length() - 1
        self.every = list(range(bits - 1, 0, -1))
        self.order = list(order)
        self.done = []
        self.terms = [(term, self.every, column) for term in (kept, taken)]
        self.rows, self.columns, self.turned = kept.shape[1], columns, turned

    def last_job(self, width, first, moving, turned):
        offset = self.columns // width

        def spec(held, column):
            def place(i, mine):
                at = 0
                for bit in held:
                    at = at * 2 + ((mine[0] >> bit) & 1)
                return at, 0, column * offset + first + (i if moving else 0)

            return pl.BlockSpec((1, self.rows, width), place)

        terms = [(term, spec(held, column)) for term, held, column in self.terms]
        shape = (self.rows, width * (2 if moving else 1))
        block = (self.rows, width)
        if turned:
            shape, block = shape[::-1], block[::-1]
        out_spec = pl.BlockSpec(block, lambda i, mine: (0, i if moving else 0))
        return terms, struct(shape), out_spec, turned

    def job(self):
        current = self.order[len(self.done)] if len(self.done) < len(self.order) else None
        done = list(self.done)

        def spec(held, column):
            left = [bit for bit in held if bit not in done and bit != current]

            def place(i, mine):
                at = 0
                for bit in held:
                    own = (mine[0] >> bit) & 1
                    if bit in done:
                        side = own
                    elif bit == current:
                        side = 1 - own
                    else:
                        side = (i >> (len(left) - 1 - left.index(bit))) & 1
                    at = at * 2 + side
                return at, 0, column

            return pl.BlockSpec((1, self.rows, self.columns), place)

        terms = [(term, spec(held, column)) for term, held, column in self.terms]
        shape = (self.rows, self.columns)
        if current is None:
            shape = shape[::-1] if self.turned else shape
            return terms, struct(shape), pl.BlockSpec(shape, lambda i, mine: (0, 0)), self.turned
        count = 2 ** (len(self.every) - len(done) - 1)
        out_spec = pl.BlockSpec((1, *shape), lambda i, mine: (i, 0, 0))
        return terms, struct((count, *shape), jnp.bfloat16), out_spec, False

    def steps(self):
        return max(1, 2 ** (len(self.every) - len(self.done) - 1))

    def send(self, given):
        bit = self.order[len(self.done)]
        arrived = exchange(given, "dp", 1 << bit)
        self.done.append(bit)
        self.terms.append((arrived, [b for b in self.every if b not in self.done], 0))


class TextScatter:
    def __init__(self, kept, taken, part):
        self.order = bit_orders()[part][1:]
        self.done = []
        self.terms = [(kept, part), (taken, part)]
        self.length = kept.shape[2]

    def job(self):
        cols = self.terms[0][0].shape[1]
        last = len(self.done) == len(self.order)
        width = self.length if last else self.length // 2

        def spec(part):
            return pl.BlockSpec((1, cols, width), lambda i, mine: (part, 0, 0 if last else 1))

        terms = [(term, spec(part)) for term, part in self.terms]
        if last:
            shape = (width, cols)
            return terms, struct(shape), pl.BlockSpec(shape, lambda i, mine: (0, 0)), True
        out_spec = pl.BlockSpec((1, cols, width), lambda i, mine: (0, 0, 0))
        return terms, struct((1, cols, width), jnp.bfloat16), out_spec, False

    def steps(self):
        return 1

    def send(self, given):
        arrived = exchange(given, "dp", 1 << self.order[len(self.done)])
        self.done.append(self.order[len(self.done)])
        self.terms.append((arrived, 0))
        self.length //= 2


def next_sums(scatters):
    results = [None] * len(scatters)
    for steps in sorted({scatter.steps() for scatter in scatters}):
        chosen = [i for i, scatter in enumerate(scatters) if scatter.steps() == steps]
        for i, result in zip(chosen, sum_stage([scatters[i].job() for i in chosen], steps)):
            results[i] = result
    return results


def send_all(scatters, given):
    for scatter, values in zip(scatters, given):
        scatter.send(values)


def bit_orders():
    bits = lax.axis_size("dp").bit_length() - 1
    return [list(range(bits)), [0] + list(range(bits - 1, 0, -1))]


def shift_ranks(pieces):
    count = lax.axis_size("tensor")
    arrived = [pieces[0]] + [None] * (count - 1)
    for m in range(1, count):
        arrived[count - m] = lax.ppermute(
            pieces[m], "tensor", [(i, (i + m) % count) for i in range(count)]
        )
    return arrived


def in_rank_order(relative):
    count = relative.shape[0]
    start = (count - lax.axis_index("tensor")) % count
    return lax.dynamic_slice_in_dim(jnp.concatenate([relative, relative], axis=0), start, count, 0)


def scatter_rows(values):
    return lax.psum_scatter(values, "tensor", scatter_dimension=0, tiled=True)


def after(values, *others):
    return lax.optimization_barrier((values, *others))[0]


def after_all(values, *others):
    return lax.optimization_barrier((values, others))[0]


def weight_gradient_plain(left, right):
    groups = lax.axis_size("dp")
    grads = right.reshape(-1, right.shape[-1])
    blocks = product(left, grads, ((0,), (1,))).astype(jnp.bfloat16)
    blocks = blocks.reshape(groups // 2, 2, -1, grads.shape[0])
    mine = lax.axis_index("dp") & 1
    return [
        lax.dynamic_index_in_dim(blocks, side, 1, keepdims=False) for side in (1 - mine, mine)
    ]


def on_device(
    tokens,
    clip_ids,
    positions,
    timesteps,
    text_states,
    text_lengths,
    out_grad,
    attn_gain,
    ffn_gain,
    query_gain,
    key_gain,
    cross_gate,
    w_query,
    w_key,
    w_value,
    w_out,
    w_text_key,
    w_text_value,
    w_ada,
    w_gate,
    w_up,
    w_down,
):
    tensor_size = lax.axis_size("tensor")
    my_rank = lax.axis_index("tensor")
    my_group = lax.axis_index("dp")
    groups = lax.axis_size("dp")
    bits = groups.bit_length() - 1
    rank = my_rank[None]
    local_rows, model_width = tokens.shape
    group_rows = local_rows * tensor_size
    head_dim = query_gain.shape[0]
    head_cols = w_query.shape[1]
    local_heads = head_cols // head_dim
    clip_count = timesteps.shape[0]
    text_len = text_states.shape[1]
    text_rows = clip_count * text_len
    hidden_cols = w_gate.shape[1]
    orders = [list(range(1, bits)), list(range(bits - 1, 0, -1))]

    tokens_all = lax.all_gather(tokens, "tensor", axis=0, tiled=True)
    embedded = time_embed(timesteps, w_ada.shape[0])
    condition = (embedded * jax.nn.sigmoid(embedded)).astype(jnp.bfloat16)
    mod_part = jnp.dot(condition, w_ada, preferred_element_type=jnp.float32)
    mod = jnp.stack(shift_ranks([mod_part] * tensor_size))
    share_rows = head_cols // groups
    share = lax.dynamic_slice_in_dim(w_out, my_group * share_rows, share_rows, 0)
    shares = jnp.stack(shift_ranks([share] * tensor_size))[None]
    shares = [shares, exchange(shares, "dp", groups // 2)]

    ids = clip_ids[:, None]
    my_ids = lax.dynamic_slice_in_dim(ids, my_rank * local_rows, local_rows)
    attn_gain_row, ffn_gain_row = attn_gain[None], ffn_gain[None]
    grad_ffn_low = gated_gradient(rank, mod, my_ids, out_grad)
    text_flat = text_states.reshape(text_rows, text_states.shape[2])
    text_key = product(w_text_key, text_flat, ((0,), (1,)))
    text_value = product(w_text_value, text_flat, ((0,), (1,)))
    gate_tanh = jnp.tanh(lax.dynamic_slice_in_dim(cross_gate, my_rank * local_heads, local_heads))
    table, text_table = clip_tables(clip_ids, text_lengths, clip_count, text_len)
    cosine, sine = rotary_tables(positions, head_dim)
    tokens_all = after(
        tokens_all, grad_ffn_low, text_key, text_value, table, text_table, cosine, sine
    )
    tokens_all, *shares = lax.optimization_barrier((tokens_all, *shares))
    shares = jnp.concatenate(shares)
    for bit in range(bits - 2, 0, -1):
        arrived = exchange(shares, "dp", 1 << bit)
        if bit > 1:
            shares = jnp.concatenate([shares, arrived])
    grad_ffn_all = lax.all_gather(grad_ffn_low, "tensor", axis=0, tiled=True)
    attn_all, qkv = project(rank, mod, ids, attn_gain_row, tokens_all, w_query, w_key, w_value)
    qkv = qkv.reshape(3 * head_cols, group_rows)
    shared = (
        rank, gate_tanh, qkv, qkv, qkv, text_key, text_value, table, text_table, cosine, sine,
        query_gain[:, None], key_gain[:, None],
    )
    mixed_heads, *kept = attention_forward(
        shared, local_heads, head_dim, clip_count, tensor_size
    )
    shares, arrived, mixed_heads = lax.optimization_barrier((shares, arrived, mixed_heads))
    shares = jnp.concatenate([shares, arrived])
    w_out_all = assemble(shares, exchange(shares, "dp", 1))
    w_out_all = w_out_all.reshape(tensor_size, head_cols, model_width)
    mixed_pieces = shift_ranks([mixed_heads[m] for m in range(tensor_size)])
    attn_out, middle, ffn_rows = middle_forward(
        rank, mod, my_ids, ffn_gain_row, tokens, w_out_all, mixed_pieces, 1
    )
    ffn_rows, grad_ffn_all = lax.optimization_barrier((ffn_rows, grad_ffn_all))
    ffn_all = lax.all_gather(ffn_rows, "tensor", axis=0, tiled=True)
    hidden, grad_gate, grad_up, back, ffn_part = feed_forward(
        ffn_all, grad_ffn_all, w_gate, w_up, w_down
    )
    grad_ffn_rows = scatter_rows(back)
    tile = min(256, hidden_cols)
    tiles = hidden_cols // tile
    rows_spec = whole_spec((group_rows, model_width))
    ffn_given, ffn_held = weight_gradient(
        [grad_ffn_all], [rows_spec], [False], [[hidden]], group_rows, model_width, 3 * hidden_cols,
        tile, lambda i: jnp.where(i < tiles // 2, tiles + i, 2 * tiles + i), [],
    )
    ffn_given, ffn_held = weight_gradient(
        [ffn_all], [rows_spec], [False], [[grad_gate], [grad_up]],
        group_rows, model_width, 3 * hidden_cols, tile,
        lambda i: jnp.where(i < tiles, i, tiles // 2 + i), [ffn_given, ffn_held],
    )
    ffn_taken = exchange(ffn_given, "dp", 1)
    ffn_scatters = [
        Scatter(ffn_held, ffn_taken, orders[part], part, 3 * hidden_cols // 2) for part in range(2)
    ]
    ffn_next = next_sums(ffn_scatters)
    grad_ffn_rows, *late = lax.optimization_barrier((grad_ffn_rows, *ffn_next))
    send_all(ffn_scatters, ffn_next)
    rows_cuts = [[grad_ffn_rows]]

    grad_middle, grad_attn_low, scale_ffn_sums, gate_attn_sums, *grad_mixed = middle_backward(
        rank, mod, my_ids, ffn_gain_row, middle, attn_out, out_grad, w_out_all, rows_cuts
    )
    grad_heads = shift_ranks(grad_mixed)
    ffn_part = after(ffn_part.reshape(group_rows, model_width), *grad_heads)
    out_cuts = [scatter_rows(ffn_part)]
    mixed_all = jnp.stack(mixed_pieces)
    out_given, out_held = weight_gradient_plain(grad_attn_low, mixed_all)
    ffn_next = next_sums(ffn_scatters)
    grad_heads, out_given, out_held, *late = lax.optimization_barrier(
        (grad_heads, out_given, out_held, *ffn_next)
    )
    send_all(ffn_scatters, ffn_next)
    out_taken = exchange(out_given, "dp", 1)
    out_scatter = Scatter(out_held, out_taken, orders[1], 0, tensor_size * head_cols)

    def send_text(grad_query, grad_text):
        given = text_gradient(grad_text, text_flat, 1)
        (out_next,) = next_sums([out_scatter])
        grad_query, given, out_next = lax.optimization_barrier((grad_query, given, out_next))
        out_scatter.send(out_next)
        return grad_query, exchange(given, "dp", 1)

    grad_qkv, grad_text, cross_sums, self_sums, text_taken = attention_backward(
        shared, grad_heads, kept, local_heads, head_dim, clip_count, send_text
    )
    rows_part, scale_attn_sums = input_rows(
        ids, tokens_all, grad_qkv, w_query, w_key, w_value, clip_count
    )
    grad_attn_rows = scatter_rows(rows_part)
    grad_text = after(grad_text, rows_part)
    text_held = text_gradient(grad_text, text_flat, 0)
    text_scatters = [TextScatter(text_held, text_taken, part) for part in range(2)]
    text_next = next_sums(text_scatters)
    grad_qkv, *text_next = lax.optimization_barrier((grad_qkv, *text_next))
    send_all(text_scatters, text_next)
    qkv_given, qkv_held = weight_gradient_plain(attn_all, grad_qkv)
    scale_attn_sums, qkv_given, qkv_held = lax.optimization_barrier(
        (scale_attn_sums, qkv_given, qkv_held)
    )
    qkv_taken = exchange(qkv_given, "dp", 1)
    qkv_scatter = Scatter(qkv_held, qkv_taken, orders[1], 0, 3 * head_cols)
    (out_ready,) = lax.optimization_barrier((out_cuts[0], qkv_given))[:1]
    block_out, gate_ffn_sums = block_result(rank, mod, my_ids, middle, out_grad, [out_ready])

    modulation = in_rank_order(mod)
    modulation = modulation.transpose(1, 0, 2).reshape(clip_count, 4, model_width)
    scale_attn, gate_attn = modulation[:, 0], jnp.tanh(modulation[:, 1])
    scale_ffn, gate_ffn = modulation[:, 2], jnp.tanh(modulation[:, 3])
    clip_mod_grad = jnp.concatenate(
        [
            scale_attn_sums * attn_gain, gate_attn_sums * (1.0 - gate_attn * gate_attn),
            scale_ffn_sums * ffn_gain, gate_ffn_sums * (1.0 - gate_ffn * gate_ffn),
        ],
        axis=1,
    )
    small_parts = (
        jnp.sum(scale_attn_sums * (1.0 + scale_attn), axis=0),
        jnp.sum(scale_ffn_sums * (1.0 + scale_ffn), axis=0),
        jnp.sum(self_sums[:, :, 0], axis=0),
        jnp.sum(self_sums[:, :, 1] + cross_sums[:, :, 0], axis=0),
        lax.dynamic_update_slice_in_dim(
            jnp.zeros((cross_gate.shape[0],), jnp.float32),
            jnp.sum(cross_sums[:, :, 1], axis=1) * (1.0 - gate_tanh * gate_tanh),
            my_rank * local_heads,
            0,
        ),
    )
    share_cols = mod_part.shape[1]
    small = jnp.concatenate(small_parts)
    small = jnp.pad(small, (0, -small.shape[0] % share_cols)).reshape(-1, share_cols)
    step_row = jnp.pad(timesteps.astype(jnp.float32), (0, share_cols - clip_count))[None]
    payloads = shift_ranks(
        [
            jnp.concatenate(
                [
                    lax.dynamic_slice_in_dim(
                        clip_mod_grad, (my_rank + m) % tensor_size * share_cols, share_cols, 1
                    ),
                    small,
                ]
            )
            for m in range(tensor_size)
        ]
    )
    (out_next,) = next_sums([out_scatter])
    qkv_next = next_sums([qkv_scatter])
    payloads, out_next, qkv_next = lax.optimization_barrier((payloads, out_next, qkv_next))
    out_scatter.send(out_next)
    send_all([qkv_scatter], qkv_next)
    summed = jnp.sum(in_rank_order(jnp.stack(payloads)), axis=0)
    mod_grad = summed[:clip_count].astype(jnp.bfloat16).astype(jnp.float32)
    mod_grad = jnp.concatenate([mod_grad, step_row])
    small = summed[clip_count:]
    small_rows = small.shape[0]
    text_next = next_sums(text_scatters)
    mod_grad, text_next = lax.optimization_barrier((mod_grad, text_next))
    send_all(text_scatters, text_next)
    for bit in range(bits):
        arrived = exchange(jnp.concatenate([small, mod_grad]), "dp", 1 << bit)
        if bit == 0:
            for _ in range(bits - 3):
                send_all(ffn_scatters, next_sums(ffn_scatters))
            ffn_terms = lax.optimization_barrier(
                ([scatter.terms[-1][0] for scatter in ffn_scatters], grad_attn_rows)
            )[0]
            for scatter, term in zip(ffn_scatters, ffn_terms):
                scatter.terms[-1] = (term, *scatter.terms[-1][1:])
            width = hidden_cols // 2
            gate_sum, up_sum, *down_sum = sum_stage(
                [
                    ffn_scatters[0].last_job(width, 0, True, False),
                    ffn_scatters[1].last_job(width, 0, True, False),
                    ffn_scatters[0].last_job(width, 2, False, True),
                    ffn_scatters[1].last_job(width, 2, False, True),
                ],
                2,
            )
            arrived, gate_sum, up_sum, down_sum = lax.optimization_barrier(
                (arrived, gate_sum, up_sum, down_sum)
            )
        if bit == 1:
            for _ in range(bits - 3):
                out_scatter.send(next_sums([out_scatter])[0])
            (out_rows,) = next_sums([out_scatter])
            qkv_next = next_sums([qkv_scatter])
            arrived, out_rows, qkv_next = lax.optimization_barrier((arrived, out_rows, qkv_next))
            send_all([qkv_scatter], qkv_next)
            out_pieces = shift_ranks(
                [
                    out_rows[:, m * head_cols : (m + 1) * head_cols].astype(jnp.bfloat16)
                    for m in range(tensor_size)
                ]
            )
        small = small + arrived[:small_rows]
        mod_grad = jnp.concatenate([mod_grad, arrived[small_rows:]])
    mod_grad = mod_grad.reshape(groups, clip_count + 1, share_cols)
    all_steps = mod_grad[:, clip_count, :clip_count].reshape(-1)
    mod_grad = mod_grad[:, :clip_count].reshape(-1, share_cols)
    cond_width = w_ada.shape[0]
    my_condition = time_columns(
        all_steps, my_group * (cond_width // groups), cond_width // groups, cond_width
    )
    finals = text_scatters + [qkv_scatter]
    for _ in range(bits - 3):
        send_all(finals, next_sums(finals))
    text_key_sum, text_value_sum, qkv_sum = next_sums(finals)
    out_sum = total(out_pieces).T
    down_sum = jnp.concatenate(down_sum, axis=0)
    qkv_sums = jnp.split(qkv_sum, 3, axis=1)
    ada_sum = product(my_condition, mod_grad.astype(jnp.bfloat16), ((0,), (0,)))
    small = small.reshape(-1)
    small_sums = []
    start = 0
    for part in small_parts:
        small_sums.append(small[start : start + part.shape[0]])
        start += part.shape[0]
    input_grad = input_result(
        rank, mod, my_ids, attn_gain_row, tokens, grad_middle, grad_attn_rows
    )
    return (
        block_out,
        input_grad,
        *small_sums,
        *qkv_sums,
        out_sum,
        text_key_sum,
        text_value_sum,
        ada_sum,
        gate_sum,
        up_sum,
        down_sum,
    )


def solution(mesh):
    return jax.shard_map(
        on_device,
        mesh=mesh,
        in_specs=(
            P(("dp", "tensor"), None),
            P("dp"),
            P("dp"),
            P("dp"),
            P("dp", None, None),
            P("dp"),
            P(("dp", "tensor"), None),
            P(),
            P(),
            P(),
            P(),
            P(),
            P(None, "tensor"),
            P(None, "tensor"),
            P(None, "tensor"),
            P("tensor", None),
            P(None, "tensor"),
            P(None, "tensor"),
            P(None, "tensor"),
            P(None, "tensor"),
            P(None, "tensor"),
            P("tensor", None),
        ),
        out_specs=(
            P(("dp", "tensor"), None),
            P(("dp", "tensor"), None),
            P(),
            P(),
            P(),
            P(),
            P(),
            P("dp", "tensor"),
            P("dp", "tensor"),
            P("dp", "tensor"),
            P("tensor", "dp"),
            P("dp", "tensor"),
            P("dp", "tensor"),
            P("dp", "tensor"),
            P("dp", "tensor"),
            P("dp", "tensor"),
            P("tensor", "dp"),
        ),
        check_vma=False,
    )
```

```python
import functools
import math

import jax
import jax.numpy as jnp
from jax import lax
from jax.experimental import pallas as pl
from jax.experimental.pallas import tpu as pltpu
from jax.sharding import PartitionSpec as P

epsilon = 1e-06


def rms_scale(values):
    return lax.rsqrt(jnp.mean(values * values, axis=-1, keepdims=True) + epsilon)


def rms_backward(grad_hat, normed, scaling):
    return scaling * (grad_hat - normed * jnp.mean(grad_hat * normed, axis=-1, keepdims=True))


def time_embed(time_steps, embed_width):
    half_width = embed_width // 2
    frequency = jnp.exp(-math.log(10000.0) * jnp.arange(half_width, dtype=jnp.float32) / half_width)
    angles = time_steps.astype(jnp.float32)[:, None] * frequency[None, :]
    return jnp.concatenate([jnp.cos(angles), jnp.sin(angles)], axis=-1)


def time_columns(time_steps, first, width, embed_width):
    half_width = embed_width // 2
    columns = first + jnp.arange(width, dtype=jnp.int32)
    frequency = jnp.exp(
        -math.log(10000.0) * (columns % half_width).astype(jnp.float32) / half_width
    )
    angles = time_steps[:, None] * frequency[None, :]
    embedded = jnp.where((columns < half_width)[None, :], jnp.cos(angles), jnp.sin(angles))
    return (embedded * jax.nn.sigmoid(embedded)).astype(jnp.bfloat16)


def exchange(values, axis_name, distance):
    count = lax.axis_size(axis_name)
    return lax.ppermute(values, axis_name, [(i, i ^ distance) for i in range(count)])


def product(left, right, contract=((1,), (0,))):
    return lax.dot_general(left, right, (contract, ((), ())), preferred_element_type=jnp.float32)


def head_norm(raw):
    return lax.rsqrt(jnp.mean(raw * raw, axis=0, keepdims=True) + epsilon)


def turn(values, cosine, sine):
    half = values.shape[0] // 2
    lead, tail = values[:half], values[half:]
    return jnp.concatenate([lead * cosine - tail * sine, lead * sine + tail * cosine], axis=0)


def turn_back(values, cosine, sine):
    half = values.shape[0] // 2
    lead, tail = values[:half], values[half:]
    return jnp.concatenate([lead * cosine + tail * sine, tail * cosine - lead * sine], axis=0)


def widen(values, extra):
    rows = values.shape[0] + extra.shape[0]
    pad = jnp.zeros((128 - rows, values.shape[1]), values.dtype)
    return jnp.concatenate([values, extra.astype(values.dtype), pad], axis=0)


def text_range(block, blocks, clips, slots):
    first = 0 if block == 0 else slots
    last = (clips if block == blocks - 1 else clips - 1) * slots
    return first, last


def total(terms):
    result = terms[0].astype(jnp.float32)
    for term in terms[1:]:
        result = result + term.astype(jnp.float32)
    return result


edge_rows = 256
apart = 2048.0
vmem_bytes = 56 << 20


def params():
    return pltpu.CompilerParams(vmem_limit_bytes=vmem_bytes)


def costs(flops, moved, transcendentals=0):
    return pl.CostEstimate(flops=flops // 64, bytes_accessed=moved // 64, transcendentals=0)


def struct(shape, kind=jnp.float32):
    return jax.ShapeDtypeStruct(shape, kind)


smem_spec = pl.BlockSpec(memory_space=pltpu.SMEM)


def whole_spec(shape):
    return pl.BlockSpec(shape, lambda *at: (0,) * len(shape))


def modulation_rows(mod, rank, which):
    count = mod.shape[0]
    per = count // 4
    shares = [mod[lax.rem(which * per + i - rank + count, count)] for i in range(per)]
    return shares[0] if per == 1 else jnp.concatenate(shares, axis=1)


def by_clip(vectors, ids):
    result = vectors[0:1]
    for clip in range(1, vectors.shape[0]):
        result = jnp.where(ids == clip, vectors[clip : clip + 1], result)
    return result


def sums_by_clip(values, ids, clips):
    return jnp.concatenate(
        [
            jnp.sum(jnp.where(ids == clip, values, 0.0), axis=0, keepdims=True)
            for clip in range(clips)
        ],
        axis=0,
    )


def gate_kernel(rank, mod, ids, out_grad, result):
    gate = by_clip(jnp.tanh(modulation_rows(mod, rank[0], 3)), ids[...])
    result[...] = (out_grad[...].astype(jnp.float32) * gate).astype(jnp.bfloat16)


def gated_gradient(rank, mod, ids, out_grad):
    return pl.pallas_call(
        gate_kernel,
        in_specs=[smem_spec] + [pl.BlockSpec(memory_space=pltpu.VMEM)] * 3,
        out_shape=struct(out_grad.shape, jnp.bfloat16),
        compiler_params=params(),
        cost_estimate=costs(out_grad.size * 4, out_grad.size * 4),
    )(rank, mod, ids, out_grad)


def project_kernel(rank, mod, ids, gain, tokens, w_query, w_key, w_value, rows_out, qkv):
    inputs = tokens[...].astype(jnp.float32)
    scaled = gain[...] * (1.0 + modulation_rows(mod, rank[0], 0))
    rows = (inputs * rms_scale(inputs) * by_clip(scaled, ids[...])).astype(jnp.bfloat16)
    rows_out[...] = rows
    for part, weight in enumerate((w_query, w_key, w_value)):
        qkv[part] = product(rows, weight[...]).T


def project(rank, mod, ids, gain, tokens_all, w_query, w_key, w_value):
    rows, width = tokens_all.shape
    cols = w_query.shape[1]
    step = edge_rows
    return pl.pallas_call(
        project_kernel,
        grid=(rows // step,),
        in_specs=[
            smem_spec, whole_spec(mod.shape), pl.BlockSpec((step, 1), lambda i: (i, 0)),
            whole_spec(gain.shape), pl.BlockSpec((step, width), lambda i: (i, 0)),
            whole_spec((width, cols)), whole_spec((width, cols)), whole_spec((width, cols)),
        ],
        out_specs=[
            pl.BlockSpec((step, width), lambda i: (i, 0)),
            pl.BlockSpec((3, cols, step), lambda i: (0, 0, i)),
        ],
        out_shape=[struct((rows, width), jnp.bfloat16), struct((3, cols, rows))],
        compiler_params=params(),
        cost_estimate=costs(6 * rows * width * cols, rows * width * 4 + 3 * cols * (width * 2 + rows * 4)),
    )(rank, mod, ids, gain, tokens_all, w_query, w_key, w_value)


def assemble_kernel(mine, held, arrived, out):
    core = mine[0] & 1
    out[:, core] = held[0]
    out[:, 1 - core] = arrived[0]


def assemble(held, arrived):
    half, ranks, rows, width = held.shape
    bits = half.bit_length() - 1

    def place(i, mine):
        pair = sum(((i >> k) & 1) << (bits - 1 - k) for k in range(bits))
        return 0, (mine[0] >> 1) ^ pair, 0, 0

    spec = pl.BlockSpec((1, ranks, rows, width), lambda i, mine: (i, 0, 0, 0))
    return pl.pallas_call(
        assemble_kernel,
        grid_spec=pltpu.PrefetchScalarGridSpec(
            num_scalar_prefetch=1,
            grid=(half,),
            in_specs=[spec, spec],
            out_specs=pl.BlockSpec((ranks, 2, rows, width), place),
        ),
        out_shape=struct((ranks, 2 * half, rows, width), held.dtype),
        compiler_params=params(),
        cost_estimate=costs(0, 0),
    )(lax.axis_index("dp")[None], held, arrived)


def middle_kernel(count, rank, mod, ids, gain, tokens, w_out, *refs):
    mixed, (attn_out, middle, *rows_out) = refs[:count], refs[count:]
    total = product(mixed[0][...], w_out[0], ((0,), (0,)))
    for m in range(1, count):
        total += product(mixed[m][...], w_out[m], ((0,), (0,)))
    attn_out[...] = total
    where_clip = ids[...]
    gate = by_clip(jnp.tanh(modulation_rows(mod, rank[0], 1)), where_clip)
    values = tokens[...].astype(jnp.float32) + gate * total
    middle[...] = values
    scaled = gain[...] * (1.0 + modulation_rows(mod, rank[0], 2))
    rows = (values * rms_scale(values) * by_clip(scaled, where_clip)).astype(jnp.bfloat16)
    step = rows.shape[0] // len(rows_out)
    for cut, ref in enumerate(rows_out):
        ref[...] = rows[cut * step : (cut + 1) * step]


def middle_forward(rank, mod, ids, gain, tokens, w_out_all, mixed, cuts):
    rows, width = tokens.shape
    vmem = pl.BlockSpec(memory_space=pltpu.VMEM)
    return pl.pallas_call(
        functools.partial(middle_kernel, len(mixed)),
        in_specs=[smem_spec] + [vmem] * (5 + len(mixed)),
        out_shape=[struct((rows, width))] * 2
        + [struct((rows // cuts, width), jnp.bfloat16)] * cuts,
        compiler_params=params(),
        cost_estimate=costs(2 * rows * w_out_all.size // 1, w_out_all.size * 2 + rows * width * 14),
    )(rank, mod, ids, gain, tokens, w_out_all, *mixed)


def middle_back_kernel(cuts, count, rank, mod, ids, gain, middle, attn_out, out_grad, w_out, *refs):
    pieces = []
    at = 0
    for terms in cuts:
        pieces.append(total([ref[...] for ref in refs[at : at + terms]]))
        at += terms
    grad_middle, grad_low, scale_sums, gate_sums = refs[at : at + 4]
    grad_mixed = refs[at + 4 :]
    clips = mod.shape[1]
    where_clip = ids[...]
    values = middle[...]
    inverse = rms_scale(values)
    normed = values * inverse
    grads = jnp.concatenate(pieces, axis=0)
    scale_sums[...] = sums_by_clip(grads * normed, where_clip, clips)
    scaled = gain[...] * (1.0 + modulation_rows(mod, rank[0], 2))
    result = out_grad[...].astype(jnp.float32) + rms_backward(
        grads * by_clip(scaled, where_clip), normed, inverse
    )
    grad_middle[...] = result
    gate = jnp.tanh(modulation_rows(mod, rank[0], 1))
    gate_sums[...] = sums_by_clip(result * attn_out[...], where_clip, clips)
    low = (result * by_clip(gate, where_clip)).astype(jnp.bfloat16)
    grad_low[...] = low
    for m in range(count):
        grad_mixed[m][...] = product(w_out[m], low, ((1,), (1,))).astype(jnp.bfloat16)


def middle_backward(rank, mod, ids, gain, middle, attn_out, out_grad, w_out_all, pieces):
    rows, width = middle.shape
    count, cols, _ = w_out_all.shape
    clips = mod.shape[1]
    vmem = pl.BlockSpec(memory_space=pltpu.VMEM)
    return pl.pallas_call(
        functools.partial(middle_back_kernel, [len(terms) for terms in pieces], count),
        in_specs=[smem_spec] + [vmem] * (7 + sum(len(terms) for terms in pieces)),
        out_shape=[
            struct((rows, width)), struct((rows, width), jnp.bfloat16),
            struct((clips, width)), struct((clips, width)),
        ]
        + [struct((cols, rows), jnp.bfloat16)] * count,
        compiler_params=params(),
        cost_estimate=costs(2 * rows * w_out_all.size, w_out_all.size * 2 + rows * width * 20),
    )(rank, mod, ids, gain, middle, attn_out, out_grad, w_out_all, *sum(pieces, []))


def ffn_kernel(rows, grads, w_gate, w_up, w_down, hidden, grad_gate, grad_up, back, out):
    gate_pre = product(rows[...], w_gate[...])
    up_pre = product(rows[...], w_up[...])
    grad_hidden = product(grads[...], w_down[...], ((1,), (1,)))
    sigmoid = 1.0 / (1.0 + jnp.exp(-gate_pre))
    silu = gate_pre * sigmoid
    hidden_low = (silu * up_pre).astype(jnp.bfloat16)
    gate_low = (grad_hidden * up_pre * (sigmoid + silu * (1.0 - sigmoid))).astype(jnp.bfloat16)
    up_low = (grad_hidden * silu).astype(jnp.bfloat16)
    hidden[...] = hidden_low
    grad_gate[...] = gate_low
    grad_up[...] = up_low
    back[...] = (
        product(gate_low, w_gate[...], ((1,), (1,))) + product(up_low, w_up[...], ((1,), (1,)))
    ).astype(jnp.bfloat16)
    out[...] = product(hidden_low, w_down[...]).astype(jnp.bfloat16)


def feed_forward(rows, grads, w_gate, w_up, w_down):
    count, width = rows.shape
    hidden = w_gate.shape[1]
    step = edge_rows
    wide = pl.BlockSpec((step, width), lambda i: (i, 0))
    inner = pl.BlockSpec((step, hidden), lambda i: (i, 0))
    return pl.pallas_call(
        ffn_kernel,
        grid=(count // step,),
        in_specs=[
            wide, wide, whole_spec(w_gate.shape), whole_spec(w_up.shape), whole_spec(w_down.shape),
        ],
        out_specs=[inner] * 3 + [wide] * 2,
        out_shape=[struct((count, hidden), jnp.bfloat16)] * 3
        + [struct((count, width), jnp.bfloat16)] * 2,
        compiler_params=params(),
        cost_estimate=costs(12 * count * width * hidden, 6 * width * hidden + 8 * count * width, count * hidden),
    )(rows, grads, w_gate, w_up, w_down)


def input_kernel(ids, tokens, grad_qkv, w_query, w_key, w_value, result, sums):
    clips = sums.shape[0]
    total = None
    for part, weight in enumerate((w_query, w_key, w_value)):
        term = lax.dot_general(
            grad_qkv[part], weight[...], (((0,), (1,)), ((), ())), preferred_element_type=jnp.float32
        )
        total = term if total is None else total + term
    result[...] = total.astype(jnp.bfloat16)
    inputs = tokens[...].astype(jnp.float32)
    found = sums_by_clip(total * (inputs * rms_scale(inputs)), ids[...], clips)

    @pl.when(pl.program_id(0) == 0)
    def _():
        sums[...] = found

    @pl.when(pl.program_id(0) > 0)
    def _():
        sums[...] += found


def input_rows(ids, tokens_all, grad_qkv, w_query, w_key, w_value, clips):
    rows, width = tokens_all.shape
    cols = w_query.shape[1]
    step = edge_rows
    return pl.pallas_call(
        input_kernel,
        grid=(rows // step,),
        in_specs=[
            pl.BlockSpec((step, 1), lambda i: (i, 0)), pl.BlockSpec((step, width), lambda i: (i, 0)),
            pl.BlockSpec((3, cols, step), lambda i: (0, 0, i)),
            whole_spec((width, cols)), whole_spec((width, cols)), whole_spec((width, cols)),
        ],
        out_specs=[pl.BlockSpec((step, width), lambda i: (i, 0)), whole_spec((clips, width))],
        out_shape=[struct((rows, width), jnp.bfloat16), struct((clips, width))],
        compiler_params=params(),
        cost_estimate=costs(6 * rows * width * cols, rows * width * 4 + 6 * cols * (width + rows)),
    )(ids, tokens_all, grad_qkv, w_query, w_key, w_value)


def block_kernel(cuts, rank, mod, ids, middle, out_grad, *refs):
    block_out, sums = refs[cuts:]
    where_clip = ids[...]
    ffn_out = jnp.concatenate([ref[...] for ref in refs[:cuts]], axis=0).astype(jnp.float32)
    gate = by_clip(jnp.tanh(modulation_rows(mod, rank[0], 3)), where_clip)
    block_out[...] = (middle[...] + gate * ffn_out).astype(jnp.bfloat16)
    sums[...] = sums_by_clip(out_grad[...].astype(jnp.float32) * ffn_out, where_clip, mod.shape[1])


def block_result(rank, mod, ids, middle, out_grad, pieces):
    vmem = pl.BlockSpec(memory_space=pltpu.VMEM)
    return pl.pallas_call(
        functools.partial(block_kernel, len(pieces)),
        in_specs=[smem_spec] + [vmem] * (4 + len(pieces)),
        out_shape=[struct(middle.shape, jnp.bfloat16), struct((mod.shape[1], middle.shape[1]))],
        compiler_params=params(),
        cost_estimate=costs(middle.size * 8, middle.size * 10),
    )(rank, mod, ids, middle, out_grad, *pieces)


def last_kernel(rank, mod, ids, gain, tokens, grad_middle, grads, result):
    inputs = tokens[...].astype(jnp.float32)
    inverse = rms_scale(inputs)
    scaled = by_clip(gain[...] * (1.0 + modulation_rows(mod, rank[0], 0)), ids[...])
    result[...] = grad_middle[...] + rms_backward(
        grads[...].astype(jnp.float32) * scaled, inputs * inverse, inverse
    )


def input_result(rank, mod, ids, gain, tokens, grad_middle, grads):
    vmem = pl.BlockSpec(memory_space=pltpu.VMEM)
    return pl.pallas_call(
        last_kernel,
        in_specs=[smem_spec] + [vmem] * 6,
        out_shape=struct(tokens.shape),
        compiler_params=params(),
        cost_estimate=costs(tokens.size * 12, tokens.size * 12),
    )(rank, mod, ids, gain, tokens, grad_middle, grads)


def weight_kernel(lefts, rights, block, mine, *refs):
    left = refs[: len(lefts)]
    right = refs[len(lefts) : len(lefts) + sum(rights)]
    given, kept, left_turned, whole = refs[-4:]
    step = pl.program_id(0)

    @pl.when(step == 0)
    def _():
        at = 0
        for ref, relative in zip(left, lefts):
            if relative:
                count = ref.shape[0]
                places = [lax.rem(mine[1] + m, count) for m in range(count)]
                values = jnp.concatenate([ref[place, 0] for place in places], axis=0)
            else:
                values = ref[...]
                values = values.reshape(-1, values.shape[-1])
            left_turned[:, at : at + values.shape[0]] = values.T
            at += values.shape[0]

    tiles = pl.num_programs(0) // len(rights)
    first = 0
    for share, count in enumerate(rights):
        chosen = right[first : first + count]
        first += count

        @pl.when(step // tiles == share)
        def _(chosen=chosen):
            at = 0
            result = None
            for ref in chosen:
                values = ref[...]
                term = product(left_turned[:, at : at + values.shape[0]], values)
                result = term if result is None else result + term
                at += values.shape[0]
            whole[...] = result.astype(jnp.bfloat16)

    for pair in range(given.shape[0]):
        for ref, side in ((given, 1 - mine[0]), (kept, mine[0])):
            start = pl.multiple_of((2 * pair + side) * block, 16)
            ref[pair] = whole[pl.ds(start, block)]


def weight_gradient(lefts, left_specs, relative, rights, depth, width, columns, tile, place, before):
    count = lax.axis_size("dp")
    mine = jnp.stack([lax.axis_index("dp") & 1, lax.axis_index("tensor")])
    block = width // count
    tiles = rights[0][0].shape[1] // tile
    out_spec = pl.BlockSpec((count // 2, block, tile), lambda i: (0, 0, place(i)))
    right_specs = [
        pl.BlockSpec(
            (ref.shape[0], tile), lambda i, share=share: (0, jnp.clip(i - share * tiles, 0, tiles - 1))
        )
        for share, refs in enumerate(rights)
        for ref in refs
    ]
    operands = [mine, *lefts, *sum(rights, []), *before]
    first = len(operands) - len(before)
    return pl.pallas_call(
        functools.partial(weight_kernel, relative, [len(refs) for refs in rights], block),
        grid=(tiles * len(rights),),
        in_specs=[smem_spec]
        + left_specs
        + right_specs
        + [pl.BlockSpec(memory_space=pl.ANY)] * len(before),
        out_specs=[out_spec] * 2,
        out_shape=[struct((count // 2, block, columns), jnp.bfloat16)] * 2,
        scratch_shapes=[pltpu.VMEM((width, depth), jnp.bfloat16), pltpu.VMEM((width, tile), jnp.bfloat16)],
        input_output_aliases={first + k: k for k in range(len(before))},
        compiler_params=params(),
        cost_estimate=costs(2 * depth * width * columns, 2 * (depth + columns) * (width + depth)),
    )(*operands)


def text_kernel(places, grads, first, second, out):
    half = grads.shape[1]
    out[0] = product(grads[0], first[...]).astype(jnp.bfloat16)
    out[1] = product(grads[1], second[...]).astype(jnp.bfloat16)


def text_gradient(grads, text_flat, side):
    count = lax.axis_size("dp")
    mine = lax.axis_index("dp")
    bits = count.bit_length() - 1
    length = text_flat.shape[1] // count
    half = count // 2
    places = []
    for order in bit_orders():
        for place in range(half):
            j = side + sum(
                1 << bit for at, bit in enumerate(order[1:]) if (place >> (bits - 2 - at)) & 1
            )
            places.append(mine ^ j)
    places = jnp.stack(places)
    cols = grads.shape[1]
    rows = text_flat.shape[0]
    return pl.pallas_call(
        text_kernel,
        grid_spec=pltpu.PrefetchScalarGridSpec(
            num_scalar_prefetch=1,
            grid=(half,),
            in_specs=[
                pl.BlockSpec(grads.shape, lambda i, at: (0, 0, 0)),
                pl.BlockSpec((rows, length), lambda i, at: (0, at[i])),
                pl.BlockSpec((rows, length), lambda i, at: (0, at[half + i])),
            ],
            out_specs=pl.BlockSpec((2, cols, length), lambda i, at: (0, 0, i)),
        ),
        out_shape=struct((2, cols, half * length), jnp.bfloat16),
        compiler_params=params(),
        cost_estimate=costs(4 * cols * rows * half * length, 4 * rows * half * length),
    )(places, grads, text_flat, text_flat)


def attend_forward(
    clips, slots, ranks, gates, query, key, value, text_key, text_value, table, text_table, cosine, sine,
    query_gain, key_gain, mixed, self_out, cross_out, self_inverse, cross_inverse,
):
    head_dim, rows = query.shape
    scale = math.log2(math.e) / math.sqrt(head_dim)
    gate = gates[pl.program_id(0)]
    raw = query[...]
    query_rot = turn(raw * head_norm(raw) * query_gain[...], cosine[...], sine[...])
    query_wide = widen(query_rot, table[0]).astype(jnp.bfloat16)
    raw = key[...]
    key_rot = turn(raw * head_norm(raw) * key_gain[...], cosine[...], sine[...])
    key_wide = widen(key_rot, table[1]).T.astype(jnp.bfloat16)
    raw = text_key[...]
    text_wide = widen(raw * head_norm(raw) * key_gain[...], text_table[...]).T.astype(jnp.bfloat16)
    ones_row = (lax.broadcasted_iota(jnp.int32, (16, rows), 0) == 0).astype(jnp.float32)
    value_wide = jnp.concatenate([value[...], ones_row], axis=0).astype(jnp.bfloat16)
    text_value_wide = jnp.concatenate(
        [text_value[...], ones_row[:, : text_value.shape[1]]], axis=0
    ).astype(jnp.bfloat16)
    blocks = rows // edge_rows
    for block in range(blocks):
        cols = slice(block * edge_rows, (block + 1) * edge_rows)
        query_blk = query_wide[:, cols]
        weights = jnp.exp2(product(key_wide, query_blk) * scale).astype(jnp.bfloat16)
        total = product(value_wide, weights)
        inverse = 1.0 / total[head_dim : head_dim + 1]
        own = total[:head_dim] * inverse
        first, last = text_range(block, blocks, clips, slots)
        weights = jnp.exp2(product(text_wide[first:last], query_blk) * scale).astype(jnp.bfloat16)
        total = product(text_value_wide[:, first:last], weights)
        text_inverse = 1.0 / total[head_dim : head_dim + 1]
        other = total[:head_dim] * text_inverse
        pieces = mixed.shape[0]
        mixed[lax.rem(block - ranks[0] + pieces, pieces)] = (own + gate * other).astype(jnp.bfloat16)
        self_out[:, cols] = own
        cross_out[:, cols] = other
        self_inverse[0, :, cols] = inverse
        cross_inverse[0, :, cols] = text_inverse


def through_norm(incoming, raw, inverse, gain):
    normed = raw * inverse
    scaled = incoming * gain
    mean = jnp.mean(scaled * normed, axis=0, keepdims=True)
    gain_part = jnp.sum(incoming * normed, axis=1, keepdims=True)
    return inverse * (scaled - normed * mean), gain_part


def rank_pieces(ranks, grads, held):
    count = len(grads)
    for m, ref in enumerate(grads):
        held[m] = ref[...].astype(jnp.float32)
    return jnp.concatenate(
        [held[lax.rem(piece - ranks[0] + count, count)] for piece in range(count)], axis=1
    )


def with_dots(weighted, out):
    rows = out.shape[1]
    low = weighted.astype(jnp.bfloat16)
    dots = jnp.sum(low.astype(jnp.float32) * out, axis=0, keepdims=True)
    high = dots.astype(jnp.bfloat16).astype(jnp.float32)
    rows_at = lax.broadcasted_iota(jnp.int32, (16, rows), 0)
    extra = jnp.where(rows_at == 0, -high, jnp.where(rows_at == 1, high - dots, 0.0))
    return widen(low.astype(jnp.float32), extra).astype(jnp.bfloat16)


def two_ones(rows):
    return (lax.broadcasted_iota(jnp.int32, (16, rows), 0) < 2).astype(jnp.float32)


def cross_backward(
    clips, slots, count, ranks, gates, query, text_key, text_value, table, text_table, cosine, sine,
    query_gain, key_gain, cross_out, cross_inverse, *refs,
):
    grad_pieces = refs[:count]
    grad_text, grad_query, gain_sums, held, text_key_sum, text_value_sum = refs[count:]
    head_dim, rows = query.shape
    scale = math.log2(math.e) / math.sqrt(head_dim)
    factor = 1.0 / math.sqrt(head_dim)
    gate = gates[pl.program_id(0)]
    raw = query[...]
    query_rot = turn(raw * head_norm(raw) * query_gain[...], cosine[...], sine[...])
    query_wide = widen(query_rot, table[0]).astype(jnp.bfloat16)
    raw = text_key[...]
    text_inv = head_norm(raw)
    text_norm = raw * text_inv * key_gain[...]
    text_low = text_norm.astype(jnp.bfloat16)
    text_wide = widen(text_norm, text_table[...]).T.astype(jnp.bfloat16)
    text_value_wide = widen(text_value[...], two_ones(text_value.shape[1])).T.astype(jnp.bfloat16)
    grads = rank_pieces(ranks, grad_pieces, held)
    cross_wide = with_dots(grads * (gate * cross_inverse[0]), cross_out[...])
    blocks = rows // edge_rows
    text_key_sum[...] = jnp.zeros_like(text_key_sum)
    text_value_sum[...] = jnp.zeros_like(text_value_sum)
    for block in range(blocks):
        cols = slice(block * edge_rows, (block + 1) * edge_rows)
        query_blk = query_wide[:, cols]
        first, last = text_range(block, blocks, clips, slots)
        grad_blk = cross_wide[:, cols]
        weights = jnp.exp2(product(text_wide[first:last], query_blk) * scale)
        slopes = (weights * product(text_value_wide[first:last], grad_blk)).astype(jnp.bfloat16)
        text_value_sum[:, first:last] += product(
            grad_blk[:head_dim], weights.astype(jnp.bfloat16), ((1,), (1,))
        )
        text_key_sum[:, first:last] += product(query_blk[:head_dim], slopes, ((1,), (1,)))
        grad_query[:, cols] = product(text_low[:, first:last], slopes)
    result, text_part = through_norm(
        text_key_sum[...] * factor, text_key[...], text_inv, key_gain[...]
    )
    grad_text[0] = result.astype(jnp.bfloat16)
    grad_text[1] = text_value_sum[...].astype(jnp.bfloat16)
    gate_part = jnp.sum(grads * cross_out[...], axis=1, keepdims=True)
    lane = lax.broadcasted_iota(jnp.int32, (head_dim, 128), 1)
    gain_sums[0] = jnp.where(lane == 0, text_part, gate_part)


def self_backward(
    count, ranks, query, key, value, table, cosine, sine, query_gain, key_gain,
    self_out, self_inverse, grad_query, *refs,
):
    grad_pieces = refs[:count]
    grad_qkv, gain_sums, held, grad_key_sum, grad_value_sum, grad_query_all = refs[count:]
    head_dim, rows = query.shape
    scale = math.log2(math.e) / math.sqrt(head_dim)
    factor = 1.0 / math.sqrt(head_dim)
    raw = query[...]
    query_inv = head_norm(raw)
    query_rot = turn(raw * query_inv * query_gain[...], cosine[...], sine[...])
    query_wide = widen(query_rot, table[0]).astype(jnp.bfloat16)
    raw = key[...]
    key_inv = head_norm(raw)
    key_rot = turn(raw * key_inv * key_gain[...], cosine[...], sine[...])
    key_low = key_rot.astype(jnp.bfloat16)
    key_wide = widen(key_rot, table[1]).T.astype(jnp.bfloat16)
    value_wide = widen(value[...], two_ones(rows)).T.astype(jnp.bfloat16)
    self_wide = with_dots(
        rank_pieces(ranks, grad_pieces, held) * self_inverse[0], self_out[...]
    )
    for block in range(rows // edge_rows):
        cols = slice(block * edge_rows, (block + 1) * edge_rows)
        query_blk = query_wide[:, cols]
        grad_blk = self_wide[:, cols]
        weights = jnp.exp2(product(key_wide, query_blk) * scale)
        slopes = (weights * product(value_wide, grad_blk)).astype(jnp.bfloat16)
        value_term = product(grad_blk[:head_dim], weights.astype(jnp.bfloat16), ((1,), (1,)))
        key_term = product(query_blk[:head_dim], slopes, ((1,), (1,)))
        if block == 0:
            grad_value_sum[...] = value_term
            grad_key_sum[...] = key_term
        else:
            grad_value_sum[...] += value_term
            grad_key_sum[...] += key_term
        grad_query_all[:, cols] = grad_query[:, cols] + product(key_low, slopes)

    incoming = turn_back(grad_query_all[...] * factor, cosine[...], sine[...])
    result, query_part = through_norm(incoming, query[...], query_inv, query_gain[...])
    grad_qkv[0] = result.astype(jnp.bfloat16)
    incoming = turn_back(grad_key_sum[...] * factor, cosine[...], sine[...])
    result, key_part = through_norm(incoming, key[...], key_inv, key_gain[...])
    grad_qkv[1] = result.astype(jnp.bfloat16)
    grad_qkv[2] = grad_value_sum[...].astype(jnp.bfloat16)
    lane = lax.broadcasted_iota(jnp.int32, (head_dim, 128), 1)
    gain_sums[0] = jnp.where(lane == 0, query_part, key_part)


def attention_specs(heads, head_dim, rows, text_rows):
    def head_block(part, width):
        return pl.BlockSpec((head_dim, width), lambda h, part=part: (part * heads + h, 0))

    return [
        smem_spec, smem_spec,
        head_block(0, rows), head_block(1, rows), head_block(2, rows),
        head_block(0, text_rows), head_block(0, text_rows),
        whole_spec((2, 16, rows)), whole_spec((16, text_rows)),
        whole_spec((head_dim // 2, rows)), whole_spec((head_dim // 2, rows)),
        whole_spec((head_dim, 1)), whole_spec((head_dim, 1)),
    ]


def attention_forward(shared, heads, head_dim, clips, ranks):
    qkv, text = shared[2], shared[5]
    rows = qkv.shape[1]
    text_rows = text.shape[1]
    cols = heads * head_dim
    hb = pl.BlockSpec((head_dim, rows), lambda h: (h, 0))
    stat = pl.BlockSpec((1, 1, rows), lambda h: (h, 0, 0))
    return pl.pallas_call(
        functools.partial(attend_forward, clips, text_rows // clips),
        grid=(heads,),
        in_specs=attention_specs(heads, head_dim, rows, text_rows),
        out_specs=[
            pl.BlockSpec((ranks, head_dim, rows // ranks), lambda h: (0, h, 0)), hb, hb, stat, stat,
        ],
        out_shape=[struct((ranks, cols, rows // ranks), jnp.bfloat16)]
        + [struct((cols, rows))] * 2
        + [struct((heads, 1, rows))] * 2,
        compiler_params=params(),
        cost_estimate=costs(8 * cols * rows * rows, cols * rows * 24, heads * rows * rows),
    )(*shared)


def attention_backward(shared, grads, kept, heads, head_dim, clips, between):
    (rank, gates, qkv, _, _, text_key, text_value, table, text_table, cosine, sine, query_gain,
     key_gain) = shared
    self_out, cross_out, self_inverse, cross_inverse = kept
    rows = qkv.shape[1]
    text_rows = text_key.shape[1]
    cols = heads * head_dim
    count = len(grads)
    (smem, _, query_s, key_s, value_s, text_key_s, text_value_s, table_s, text_table_s, cos_s,
     sin_s, query_gain_s, key_gain_s) = attention_specs(heads, head_dim, rows, text_rows)
    hb = pl.BlockSpec((head_dim, rows), lambda h: (h, 0))
    stat = pl.BlockSpec((1, 1, rows), lambda h: (h, 0, 0))
    sums = pl.BlockSpec((1, head_dim, 128), lambda h: (h, 0, 0))
    grad_specs = [pl.BlockSpec((head_dim, rows // count), lambda h: (h, 0))] * count
    held = pltpu.VMEM((count, head_dim, rows // count), jnp.float32)
    grad_text, grad_query, cross_sums = pl.pallas_call(
        functools.partial(cross_backward, clips, text_rows // clips, count),
        grid=(heads,),
        in_specs=[
            smem, smem, query_s, text_key_s, text_value_s, table_s, text_table_s, cos_s, sin_s,
            query_gain_s, key_gain_s, hb, stat, *grad_specs,
        ],
        out_specs=[pl.BlockSpec((2, head_dim, text_rows), lambda h: (0, h, 0)), hb, sums],
        out_shape=[
            struct((2, cols, text_rows), jnp.bfloat16), struct((cols, rows)),
            struct((heads, head_dim, 128)),
        ],
        scratch_shapes=[held] + [pltpu.VMEM((head_dim, text_rows), jnp.float32)] * 2,
        compiler_params=params(),
        cost_estimate=costs(6 * cols * rows * text_rows, cols * rows * 14, heads * rows * text_rows // 2),
    )(rank, gates, qkv, text_key, text_value, table, text_table, cosine, sine, query_gain, key_gain,
      cross_out, cross_inverse, *grads)
    grad_query, passed = between(grad_query, grad_text)
    grad_qkv, self_sums = pl.pallas_call(
        functools.partial(self_backward, count),
        grid=(heads,),
        in_specs=[
            smem, query_s, key_s, value_s, table_s, cos_s, sin_s, query_gain_s, key_gain_s,
            hb, stat, hb, *grad_specs,
        ],
        out_specs=[pl.BlockSpec((3, head_dim, rows), lambda h: (0, h, 0)), sums],
        out_shape=[struct((3, cols, rows), jnp.bfloat16), struct((heads, head_dim, 128))],
        scratch_shapes=[held] + [pltpu.VMEM((head_dim, rows), jnp.float32)] * 3,
        compiler_params=params(),
        cost_estimate=costs(20 * cols * rows * rows, cols * rows * 24, heads * rows * rows),
    )(rank, qkv, qkv, qkv, table, cosine, sine, query_gain, key_gain, self_out, self_inverse,
      grad_query, *grads)
    return grad_qkv, grad_text, cross_sums, self_sums, passed


def clip_tables(clip_ids, text_lengths, clips, slots):
    rows = clip_ids.shape[0]
    feature = jnp.arange(16, dtype=jnp.int32)[:, None]
    member = feature == clip_ids[None, :]
    query_part = jnp.where(feature < clips, jnp.where(member, 0.0, -apart), jnp.where(feature == clips, -apart, 0.0))
    key_part = member.astype(jnp.float32)
    owner = jnp.repeat(jnp.arange(clips, dtype=jnp.int32), slots)
    slot = jnp.tile(jnp.arange(slots, dtype=jnp.int32), clips)
    dead = slot >= jnp.repeat(text_lengths, slots)
    text_part = jnp.where(feature == clips, dead[None, :], feature == owner[None, :]).astype(jnp.float32)
    return jnp.stack([query_part, key_part]), text_part


def rotary_tables(positions, head_dim):
    half = head_dim // 2
    frequency = jnp.exp(-math.log(10000.0) * jnp.arange(half, dtype=jnp.float32) * 2.0 / head_dim)
    angles = frequency[:, None] * positions.astype(jnp.float32)[None, :]
    return jnp.cos(angles), jnp.sin(angles)


def sum_kernel(jobs, mine, *refs):
    at = 0
    outs = refs[sum(count for count, _ in jobs) :]
    for (count, turned), out in zip(jobs, outs):
        value = total([ref[0] for ref in refs[at : at + count]])
        value = value.T if turned else value
        if len(out.shape) == 3:
            out[0] = value.astype(out.dtype)
        else:
            out[...] = value.astype(out.dtype)
        at += count


def sum_stage(jobs, steps):
    mine = lax.axis_index("dp")[None]
    terms = [term for job in jobs for term, _ in job[0]]
    return pl.pallas_call(
        functools.partial(sum_kernel, [(len(job[0]), job[3]) for job in jobs]),
        grid_spec=pltpu.PrefetchScalarGridSpec(
            num_scalar_prefetch=1,
            grid=(steps,),
            in_specs=[spec for job in jobs for _, spec in job[0]],
            out_specs=[job[2] for job in jobs],
        ),
        out_shape=[job[1] for job in jobs],
        compiler_params=params(),
        cost_estimate=costs(0, 0),
    )(mine, *terms)


class Scatter:
    def __init__(self, kept, taken, order, column, columns, turned=False):
        bits = lax.axis_size("dp").bit_length() - 1
        self.every = list(range(bits - 1, 0, -1))
        self.order = list(order)
        self.done = []
        self.terms = [(term, self.every, column) for term in (kept, taken)]
        self.rows, self.columns, self.turned = kept.shape[1], columns, turned

    def last_job(self, width, first, moving, turned):
        offset = self.columns // width

        def spec(held, column):
            def place(i, mine):
                at = 0
                for bit in held:
                    at = at * 2 + ((mine[0] >> bit) & 1)
                return at, 0, column * offset + first + (i if moving else 0)

            return pl.BlockSpec((1, self.rows, width), place)

        terms = [(term, spec(held, column)) for term, held, column in self.terms]
        shape = (self.rows, width * (2 if moving else 1))
        block = (self.rows, width)
        if turned:
            shape, block = shape[::-1], block[::-1]
        out_spec = pl.BlockSpec(block, lambda i, mine: (0, i if moving else 0))
        return terms, struct(shape), out_spec, turned

    def job(self):
        current = self.order[len(self.done)] if len(self.done) < len(self.order) else None
        done = list(self.done)

        def spec(held, column):
            left = [bit for bit in held if bit not in done and bit != current]

            def place(i, mine):
                at = 0
                for bit in held:
                    own = (mine[0] >> bit) & 1
                    if bit in done:
                        side = own
                    elif bit == current:
                        side = 1 - own
                    else:
                        side = (i >> (len(left) - 1 - left.index(bit))) & 1
                    at = at * 2 + side
                return at, 0, column

            return pl.BlockSpec((1, self.rows, self.columns), place)

        terms = [(term, spec(held, column)) for term, held, column in self.terms]
        shape = (self.rows, self.columns)
        if current is None:
            shape = shape[::-1] if self.turned else shape
            return terms, struct(shape), pl.BlockSpec(shape, lambda i, mine: (0, 0)), self.turned
        count = 2 ** (len(self.every) - len(done) - 1)
        out_spec = pl.BlockSpec((1, *shape), lambda i, mine: (i, 0, 0))
        return terms, struct((count, *shape), jnp.bfloat16), out_spec, False

    def steps(self):
        return max(1, 2 ** (len(self.every) - len(self.done) - 1))

    def send(self, given):
        bit = self.order[len(self.done)]
        arrived = exchange(given, "dp", 1 << bit)
        self.done.append(bit)
        self.terms.append((arrived, [b for b in self.every if b not in self.done], 0))


class TextScatter:
    def __init__(self, kept, taken, part):
        self.order = bit_orders()[part][1:]
        self.done = []
        self.terms = [(kept, part), (taken, part)]
        self.length = kept.shape[2]

    def job(self):
        cols = self.terms[0][0].shape[1]
        last = len(self.done) == len(self.order)
        width = self.length if last else self.length // 2

        def spec(part):
            return pl.BlockSpec((1, cols, width), lambda i, mine: (part, 0, 0 if last else 1))

        terms = [(term, spec(part)) for term, part in self.terms]
        if last:
            shape = (width, cols)
            return terms, struct(shape), pl.BlockSpec(shape, lambda i, mine: (0, 0)), True
        out_spec = pl.BlockSpec((1, cols, width), lambda i, mine: (0, 0, 0))
        return terms, struct((1, cols, width), jnp.bfloat16), out_spec, False

    def steps(self):
        return 1

    def send(self, given):
        arrived = exchange(given, "dp", 1 << self.order[len(self.done)])
        self.done.append(self.order[len(self.done)])
        self.terms.append((arrived, 0))
        self.length //= 2


def next_sums(scatters):
    results = [None] * len(scatters)
    for steps in sorted({scatter.steps() for scatter in scatters}):
        chosen = [i for i, scatter in enumerate(scatters) if scatter.steps() == steps]
        for i, result in zip(chosen, sum_stage([scatters[i].job() for i in chosen], steps)):
            results[i] = result
    return results


def send_all(scatters, given):
    for scatter, values in zip(scatters, given):
        scatter.send(values)


def bit_orders():
    bits = lax.axis_size("dp").bit_length() - 1
    return [list(range(bits)), [0] + list(range(bits - 1, 0, -1))]


def shift_ranks(pieces):
    count = lax.axis_size("tensor")
    arrived = [pieces[0]] + [None] * (count - 1)
    for m in range(1, count):
        arrived[count - m] = lax.ppermute(
            pieces[m], "tensor", [(i, (i + m) % count) for i in range(count)]
        )
    return arrived


def in_rank_order(relative):
    count = relative.shape[0]
    start = (count - lax.axis_index("tensor")) % count
    return lax.dynamic_slice_in_dim(jnp.concatenate([relative, relative], axis=0), start, count, 0)


def scatter_rows(values):
    return lax.psum_scatter(values, "tensor", scatter_dimension=0, tiled=True)


def after(values, *others):
    return lax.optimization_barrier((values, *others))[0]


def after_all(values, *others):
    return lax.optimization_barrier((values, others))[0]


def weight_gradient_plain(left, right):
    groups = lax.axis_size("dp")
    grads = right.reshape(-1, right.shape[-1])
    blocks = product(left, grads, ((0,), (1,))).astype(jnp.bfloat16)
    blocks = blocks.reshape(groups // 2, 2, -1, grads.shape[0])
    mine = lax.axis_index("dp") & 1
    return [
        lax.dynamic_index_in_dim(blocks, side, 1, keepdims=False) for side in (1 - mine, mine)
    ]


def on_device(
    tokens,
    clip_ids,
    positions,
    timesteps,
    text_states,
    text_lengths,
    out_grad,
    attn_gain,
    ffn_gain,
    query_gain,
    key_gain,
    cross_gate,
    w_query,
    w_key,
    w_value,
    w_out,
    w_text_key,
    w_text_value,
    w_ada,
    w_gate,
    w_up,
    w_down,
):
    tensor_size = lax.axis_size("tensor")
    my_rank = lax.axis_index("tensor")
    my_group = lax.axis_index("dp")
    groups = lax.axis_size("dp")
    bits = groups.bit_length() - 1
    rank = my_rank[None]
    local_rows, model_width = tokens.shape
    group_rows = local_rows * tensor_size
    head_dim = query_gain.shape[0]
    head_cols = w_query.shape[1]
    local_heads = head_cols // head_dim
    clip_count = timesteps.shape[0]
    text_len = text_states.shape[1]
    text_rows = clip_count * text_len
    hidden_cols = w_gate.shape[1]
    orders = [list(range(1, bits)), list(range(bits - 1, 0, -1))]

    tokens_all = lax.all_gather(tokens, "tensor", axis=0, tiled=True)
    embedded = time_embed(timesteps, w_ada.shape[0])
    condition = (embedded * jax.nn.sigmoid(embedded)).astype(jnp.bfloat16)
    mod_part = jnp.dot(condition, w_ada, preferred_element_type=jnp.float32)
    mod = jnp.stack(shift_ranks([mod_part] * tensor_size))
    share_rows = head_cols // groups
    share = lax.dynamic_slice_in_dim(w_out, my_group * share_rows, share_rows, 0)
    shares = jnp.stack(shift_ranks([share] * tensor_size))[None]
    shares = [shares, exchange(shares, "dp", groups // 2)]

    ids = clip_ids[:, None]
    my_ids = lax.dynamic_slice_in_dim(ids, my_rank * local_rows, local_rows)
    attn_gain_row, ffn_gain_row = attn_gain[None], ffn_gain[None]
    grad_ffn_low = gated_gradient(rank, mod, my_ids, out_grad)
    text_flat = text_states.reshape(text_rows, text_states.shape[2])
    text_key = product(w_text_key, text_flat, ((0,), (1,)))
    text_value = product(w_text_value, text_flat, ((0,), (1,)))
    gate_tanh = jnp.tanh(lax.dynamic_slice_in_dim(cross_gate, my_rank * local_heads, local_heads))
    table, text_table = clip_tables(clip_ids, text_lengths, clip_count, text_len)
    cosine, sine = rotary_tables(positions, head_dim)
    tokens_all = after(
        tokens_all, grad_ffn_low, text_key, text_value, table, text_table, cosine, sine
    )
    tokens_all, *shares = lax.optimization_barrier((tokens_all, *shares))
    shares = jnp.concatenate(shares)
    for bit in range(bits - 2, 0, -1):
        arrived = exchange(shares, "dp", 1 << bit)
        if bit > 1:
            shares = jnp.concatenate([shares, arrived])
    grad_ffn_all = lax.all_gather(grad_ffn_low, "tensor", axis=0, tiled=True)
    attn_all, qkv = project(rank, mod, ids, attn_gain_row, tokens_all, w_query, w_key, w_value)
    qkv = qkv.reshape(3 * head_cols, group_rows)
    shared = (
        rank, gate_tanh, qkv, qkv, qkv, text_key, text_value, table, text_table, cosine, sine,
        query_gain[:, None], key_gain[:, None],
    )
    mixed_heads, *kept = attention_forward(
        shared, local_heads, head_dim, clip_count, tensor_size
    )
    shares, arrived, mixed_heads = lax.optimization_barrier((shares, arrived, mixed_heads))
    shares = jnp.concatenate([shares, arrived])
    w_out_all = assemble(shares, exchange(shares, "dp", 1))
    w_out_all = w_out_all.reshape(tensor_size, head_cols, model_width)
    mixed_pieces = shift_ranks([mixed_heads[m] for m in range(tensor_size)])
    attn_out, middle, ffn_rows = middle_forward(
        rank, mod, my_ids, ffn_gain_row, tokens, w_out_all, mixed_pieces, 1
    )
    ffn_rows, grad_ffn_all = lax.optimization_barrier((ffn_rows, grad_ffn_all))
    ffn_all = lax.all_gather(ffn_rows, "tensor", axis=0, tiled=True)
    hidden, grad_gate, grad_up, back, ffn_part = feed_forward(
        ffn_all, grad_ffn_all, w_gate, w_up, w_down
    )
    grad_ffn_rows = scatter_rows(back)
    tile = min(256, hidden_cols)
    tiles = hidden_cols // tile
    rows_spec = whole_spec((group_rows, model_width))
    ffn_given, ffn_held = weight_gradient(
        [grad_ffn_all], [rows_spec], [False], [[hidden]], group_rows, model_width, 3 * hidden_cols,
        tile, lambda i: jnp.where(i < tiles // 2, tiles + i, 2 * tiles + i), [],
    )
    ffn_given, ffn_held = weight_gradient(
        [ffn_all], [rows_spec], [False], [[grad_gate], [grad_up]],
        group_rows, model_width, 3 * hidden_cols, tile,
        lambda i: jnp.where(i < tiles, i, tiles // 2 + i), [ffn_given, ffn_held],
    )
    ffn_taken = exchange(ffn_given, "dp", 1)
    ffn_scatters = [
        Scatter(ffn_held, ffn_taken, orders[part], part, 3 * hidden_cols // 2) for part in range(2)
    ]
    ffn_next = next_sums(ffn_scatters)
    grad_ffn_rows, *late = lax.optimization_barrier((grad_ffn_rows, *ffn_next))
    send_all(ffn_scatters, ffn_next)
    rows_cuts = [[grad_ffn_rows]]

    grad_middle, grad_attn_low, scale_ffn_sums, gate_attn_sums, *grad_mixed = middle_backward(
        rank, mod, my_ids, ffn_gain_row, middle, attn_out, out_grad, w_out_all, rows_cuts
    )
    grad_heads = shift_ranks(grad_mixed)
    ffn_part = after(ffn_part.reshape(group_rows, model_width), *grad_heads)
    out_cuts = [scatter_rows(ffn_part)]
    mixed_all = jnp.stack(mixed_pieces)
    out_given, out_held = weight_gradient_plain(grad_attn_low, mixed_all)
    ffn_next = next_sums(ffn_scatters)
    grad_heads, out_given, out_held, *late = lax.optimization_barrier(
        (grad_heads, out_given, out_held, *ffn_next)
    )
    send_all(ffn_scatters, ffn_next)
    out_taken = exchange(out_given, "dp", 1)
    out_scatter = Scatter(out_held, out_taken, orders[1], 0, tensor_size * head_cols)

    def send_text(grad_query, grad_text):
        given = text_gradient(grad_text, text_flat, 1)
        (out_next,) = next_sums([out_scatter])
        grad_query, given, out_next = lax.optimization_barrier((grad_query, given, out_next))
        out_scatter.send(out_next)
        return grad_query, exchange(given, "dp", 1)

    grad_qkv, grad_text, cross_sums, self_sums, text_taken = attention_backward(
        shared, grad_heads, kept, local_heads, head_dim, clip_count, send_text
    )
    rows_part, scale_attn_sums = input_rows(
        ids, tokens_all, grad_qkv, w_query, w_key, w_value, clip_count
    )
    grad_attn_rows = scatter_rows(rows_part)
    grad_text = after(grad_text, rows_part)
    text_held = text_gradient(grad_text, text_flat, 0)
    text_scatters = [TextScatter(text_held, text_taken, part) for part in range(2)]
    text_next = next_sums(text_scatters)
    grad_qkv, *text_next = lax.optimization_barrier((grad_qkv, *text_next))
    send_all(text_scatters, text_next)
    qkv_given, qkv_held = weight_gradient_plain(attn_all, grad_qkv)
    scale_attn_sums, qkv_given, qkv_held = lax.optimization_barrier(
        (scale_attn_sums, qkv_given, qkv_held)
    )
    qkv_taken = exchange(qkv_given, "dp", 1)
    qkv_scatter = Scatter(qkv_held, qkv_taken, orders[1], 0, 3 * head_cols)
    (out_next,) = next_sums([out_scatter])
    out_ready, out_next = lax.optimization_barrier((out_cuts[0], out_next))
    out_scatter.send(out_next)
    block_out, gate_ffn_sums = block_result(rank, mod, my_ids, middle, out_grad, [out_ready])

    modulation = in_rank_order(mod)
    modulation = modulation.transpose(1, 0, 2).reshape(clip_count, 4, model_width)
    scale_attn, gate_attn = modulation[:, 0], jnp.tanh(modulation[:, 1])
    scale_ffn, gate_ffn = modulation[:, 2], jnp.tanh(modulation[:, 3])
    clip_mod_grad = jnp.concatenate(
        [
            scale_attn_sums * attn_gain, gate_attn_sums * (1.0 - gate_attn * gate_attn),
            scale_ffn_sums * ffn_gain, gate_ffn_sums * (1.0 - gate_ffn * gate_ffn),
        ],
        axis=1,
    )
    small_parts = (
        jnp.sum(scale_attn_sums * (1.0 + scale_attn), axis=0),
        jnp.sum(scale_ffn_sums * (1.0 + scale_ffn), axis=0),
        jnp.sum(self_sums[:, :, 0], axis=0),
        jnp.sum(self_sums[:, :, 1] + cross_sums[:, :, 0], axis=0),
        lax.dynamic_update_slice_in_dim(
            jnp.zeros((cross_gate.shape[0],), jnp.float32),
            jnp.sum(cross_sums[:, :, 1], axis=1) * (1.0 - gate_tanh * gate_tanh),
            my_rank * local_heads,
            0,
        ),
    )
    share_cols = mod_part.shape[1]
    small = jnp.concatenate(small_parts)
    small = jnp.pad(small, (0, -small.shape[0] % share_cols)).reshape(-1, share_cols)
    step_row = jnp.pad(timesteps.astype(jnp.float32), (0, share_cols - clip_count))[None]
    payloads = shift_ranks(
        [
            jnp.concatenate(
                [
                    lax.dynamic_slice_in_dim(
                        clip_mod_grad, (my_rank + m) % tensor_size * share_cols, share_cols, 1
                    ),
                    small,
                ]
            )
            for m in range(tensor_size)
        ]
    )
    qkv_next = next_sums([qkv_scatter])
    payloads, qkv_next = lax.optimization_barrier((payloads, qkv_next))
    send_all([qkv_scatter], qkv_next)
    summed = jnp.sum(in_rank_order(jnp.stack(payloads)), axis=0)
    mod_grad = summed[:clip_count].astype(jnp.bfloat16).astype(jnp.float32)
    mod_grad = jnp.concatenate([mod_grad, step_row])
    small = summed[clip_count:]
    small_rows = small.shape[0]
    text_next = next_sums(text_scatters)
    mod_grad, text_next = lax.optimization_barrier((mod_grad, text_next))
    send_all(text_scatters, text_next)
    for bit in range(bits):
        arrived = exchange(jnp.concatenate([small, mod_grad]), "dp", 1 << bit)
        if bit == 0:
            for _ in range(bits - 3):
                send_all(ffn_scatters, next_sums(ffn_scatters))
            ffn_terms = lax.optimization_barrier(
                ([scatter.terms[-1][0] for scatter in ffn_scatters], grad_attn_rows)
            )[0]
            for scatter, term in zip(ffn_scatters, ffn_terms):
                scatter.terms[-1] = (term, *scatter.terms[-1][1:])
            width = hidden_cols // 2
            gate_sum, up_sum, *down_sum = sum_stage(
                [
                    ffn_scatters[0].last_job(width, 0, True, False),
                    ffn_scatters[1].last_job(width, 0, True, False),
                    ffn_scatters[0].last_job(width, 2, False, True),
                    ffn_scatters[1].last_job(width, 2, False, True),
                ],
                2,
            )
            arrived, gate_sum, up_sum, down_sum = lax.optimization_barrier(
                (arrived, gate_sum, up_sum, down_sum)
            )
        if bit == 1:
            for _ in range(bits - 3):
                out_scatter.send(next_sums([out_scatter])[0])
            (out_rows,) = next_sums([out_scatter])
            qkv_next = next_sums([qkv_scatter])
            arrived, out_rows, qkv_next = lax.optimization_barrier((arrived, out_rows, qkv_next))
            send_all([qkv_scatter], qkv_next)
            out_pieces = shift_ranks(
                [
                    out_rows[:, m * head_cols : (m + 1) * head_cols].astype(jnp.bfloat16)
                    for m in range(tensor_size)
                ]
            )
        small = small + arrived[:small_rows]
        mod_grad = jnp.concatenate([mod_grad, arrived[small_rows:]])
    mod_grad = mod_grad.reshape(groups, clip_count + 1, share_cols)
    all_steps = mod_grad[:, clip_count, :clip_count].reshape(-1)
    mod_grad = mod_grad[:, :clip_count].reshape(-1, share_cols)
    cond_width = w_ada.shape[0]
    my_condition = time_columns(
        all_steps, my_group * (cond_width // groups), cond_width // groups, cond_width
    )
    finals = text_scatters + [qkv_scatter]
    for _ in range(bits - 3):
        send_all(finals, next_sums(finals))
    text_key_sum, text_value_sum, qkv_sum = next_sums(finals)
    out_sum = total(out_pieces).T
    down_sum = jnp.concatenate(down_sum, axis=0)
    qkv_sums = jnp.split(qkv_sum, 3, axis=1)
    ada_sum = product(my_condition, mod_grad.astype(jnp.bfloat16), ((0,), (0,)))
    small = small.reshape(-1)
    small_sums = []
    start = 0
    for part in small_parts:
        small_sums.append(small[start : start + part.shape[0]])
        start += part.shape[0]
    input_grad = input_result(
        rank, mod, my_ids, attn_gain_row, tokens, grad_middle, grad_attn_rows
    )
    return (
        block_out,
        input_grad,
        *small_sums,
        *qkv_sums,
        out_sum,
        text_key_sum,
        text_value_sum,
        ada_sum,
        gate_sum,
        up_sum,
        down_sum,
    )


def solution(mesh):
    return jax.shard_map(
        on_device,
        mesh=mesh,
        in_specs=(
            P(("dp", "tensor"), None),
            P("dp"),
            P("dp"),
            P("dp"),
            P("dp", None, None),
            P("dp"),
            P(("dp", "tensor"), None),
            P(),
            P(),
            P(),
            P(),
            P(),
            P(None, "tensor"),
            P(None, "tensor"),
            P(None, "tensor"),
            P("tensor", None),
            P(None, "tensor"),
            P(None, "tensor"),
            P(None, "tensor"),
            P(None, "tensor"),
            P(None, "tensor"),
            P("tensor", None),
        ),
        out_specs=(
            P(("dp", "tensor"), None),
            P(("dp", "tensor"), None),
            P(),
            P(),
            P(),
            P(),
            P(),
            P("dp", "tensor"),
            P("dp", "tensor"),
            P("dp", "tensor"),
            P("tensor", "dp"),
            P("dp", "tensor"),
            P("dp", "tensor"),
            P("dp", "tensor"),
            P("dp", "tensor"),
            P("dp", "tensor"),
            P("tensor", "dp"),
        ),
        check_vma=False,
    )
```
